32 devices in a mesh: group: 4 (over y, core), pair: 8 (over z, x).
Axes of the slice: x: 2, y: 2, z: 4, core: 2. Of those that a mesh axis runs over, the one named last changes fastest.
Arguments:
- genotypes: int32 [4096, 16384], P(None, ('group', 'pair')), may hold values from 0 to 2, as said below
- dest_group: int32 [64], replicated, may hold values from 0 to 3, as said below
Outputs:
- rotated: bfloat16 [4096, 16384], P(None, ('group', 'pair'))
The draws below stay inside these ranges and needn't reach their ends.
Inputs may be any that keep to these rules, and one draw needn't show every extreme that they name: For every pair index p and side k there is an offset s with dest_group[(g * 8 + p) * 2 + k] = (g + s) mod 4 for all g, and the two sides have different offsets; so every position (t, p, k) receives exactly one block. `genotypes`: allele counts of two alleles.
All inputs are finite; a program needn't handle non-finite values.
Results may differ from the reference program's by a relative error of at most 0.0077.
Values may be sent and summed in bfloat16 or wider, within the bound.
No kernel may reach another device: no remote copies, remote signals or barrier semaphores. Data moves between devices by JAX's collectives and lax.ppermute only.
A program may use at most 128 MiB of HBM per device.

```python
import jax
import jax.numpy as jnp
from jax import lax

INDIV = 4096
BLOCK = 256
ROUNDS = 3
GROUPS = 4
PAIRS = 8
NBLK = 64
NSNP = 16384


def draw_haplotype(key, indiv_freq):
    key_fresh = jax.random.fold_in(key, 1)
    key_switch = jax.random.fold_in(key, 2)
    fresh = jax.random.randint(key_fresh, (INDIV, NSNP), 0, 1000)
    switch = jax.random.randint(key_switch, (INDIV, NSNP), 0, 1000) < 400
    snp_iota = lax.broadcasted_iota(jnp.int32, (INDIV, NSNP), 1)
    marks = jnp.where(switch, snp_iota, 0).astype(jnp.int32)
    source = lax.cummax(marks, axis=1).astype(jnp.int32)
    copied = jnp.take_along_axis(fresh, source, axis=1)
    return (copied < indiv_freq).astype(jnp.int32)


def draw_genotypes(key, part):
    key_freq = jax.random.fold_in(key, 11)
    key_shift = jax.random.fold_in(key, 12)
    key_ancestry = jax.random.fold_in(key, 13)
    key_first = jax.random.fold_in(key, 14)
    key_second = jax.random.fold_in(key, 15)
    base_level = jax.random.randint(key_freq, (1, NSNP), 100, 901)
    pop_shift = jax.random.randint(key_shift, (4, NSNP), -150, 151)
    pop_freq = jnp.clip(base_level + pop_shift, 20, 980).astype(jnp.int32)
    ancestry = jax.random.randint(key_ancestry, (INDIV,), 0, 4).astype(jnp.int32)
    indiv_freq = pop_freq[ancestry]
    first_allele = draw_haplotype(key_first, indiv_freq)
    second_allele = draw_haplotype(key_second, indiv_freq)
    return (first_allele + second_allele).astype(jnp.int32)


def draw_dest_group(key, part):
    key_side0 = jax.random.fold_in(key, 21)
    key_side1 = jax.random.fold_in(key, 22)
    offset_zero = jax.random.randint(key_side0, (PAIRS,), 0, GROUPS)
    offset_one = (offset_zero + jax.random.randint(key_side1, (PAIRS,), 1, GROUPS)) % GROUPS
    groups_iota = jnp.arange(GROUPS, dtype=jnp.int32)[:, None]
    dest_zero = (groups_iota + offset_zero[None, :]) % GROUPS
    dest_one = (groups_iota + offset_one[None, :]) % GROUPS
    return jnp.stack([dest_zero, dest_one], axis=-1).reshape(NBLK).astype(jnp.int32)


def setup_inputs(seed: int = 0) -> dict:
    streams_of = jax.random.split(jax.random.key(seed), 3)
    genotypes = draw_genotypes(jax.random.fold_in(streams_of[2], 71), 0)
    dest_group = draw_dest_group(jax.random.fold_in(streams_of[2], 71), 0)
    return {"genotypes": genotypes, "dest_group": dest_group}


epsilon = 1e-05

def standardize(counts):
    values = counts.astype(jnp.float32)
    col_mean = lax.optimization_barrier(jnp.mean(values, axis=0))
    centred = values - col_mean
    col_var = lax.optimization_barrier(jnp.mean(centred * centred, axis=0))
    return (centred / jnp.sqrt(col_var + epsilon)).astype(jnp.bfloat16)

def rotation_for(top_block, low_block):
    blk_width = top_block.shape[1]
    top_wide = top_block.astype(jnp.float32)
    low_wide = low_block.astype(jnp.float32)
    norm_top = lax.optimization_barrier(jnp.sum(top_wide * top_wide, axis=0))
    norm_low = lax.optimization_barrier(jnp.sum(low_wide * low_wide, axis=0))
    cross_gram = lax.dot_general(top_block.astype(jnp.float32), low_block.astype(jnp.float32), (((0,), (0,)), ((), ())), preferred_element_type=jnp.float32)
    coupling = 2.0 * cross_gram / (norm_top[:, None] + norm_low[None, :] + epsilon)
    zero_block = jnp.zeros((blk_width, blk_width), jnp.float32)
    skew_part = jnp.concatenate([jnp.concatenate([zero_block, coupling], axis=1), jnp.concatenate([-coupling.T, zero_block], axis=1)], axis=0)
    identity = jnp.eye(2 * blk_width, dtype=jnp.float32)
    gram_matrix = identity + jnp.dot(skew_part.T, skew_part, precision=lax.Precision.HIGHEST)
    factor = jnp.linalg.cholesky(gram_matrix)
    lifted = identity + skew_part
    rotation = jax.scipy.linalg.solve_triangular(factor, lifted.T, lower=True).T
    return rotation.astype(jnp.bfloat16)

def apply_pair(top_block, low_block):
    rotation = rotation_for(top_block, low_block)
    joined = jnp.concatenate([top_block, low_block], axis=1)
    result = jnp.dot(joined.astype(jnp.float32), rotation.astype(jnp.float32), preferred_element_type=jnp.float32).astype(jnp.bfloat16)
    return (result[:, :BLOCK], result[:, BLOCK:])

def reference(genotypes, dest_group):
    counts = genotypes.reshape(INDIV, GROUPS, PAIRS * 2 * BLOCK)
    counts = jnp.moveaxis(counts, 1, 0)
    scaled = lax.map(standardize, counts)
    scaled = scaled.reshape(GROUPS, INDIV, PAIRS, 2, BLOCK)
    scaled = jnp.transpose(scaled, (0, 2, 3, 1, 4))
    dest_table = dest_group.reshape(GROUPS, PAIRS, 2)
    groups_iota = jnp.arange(GROUPS, dtype=jnp.int32)
    matches = (dest_table[None, :, :, :] == groups_iota[:, None, None, None]).astype(jnp.int32)
    source = lax.optimization_barrier(jnp.sum(matches * groups_iota[None, :, None, None], axis=1)).astype(jnp.int32)
    pair_iota = jnp.arange(PAIRS, dtype=jnp.int32)[None, :, None]
    side_iota = jnp.arange(2, dtype=jnp.int32)[None, None, :]
    placed = scaled[source, pair_iota, side_iota]
    top_all = placed[:, :, 0]
    low_all = placed[:, :, 1]
    group_step = jax.vmap(apply_pair)
    for cycle_round in range(ROUNDS):
        top_all, low_new = lax.map(lambda pieces: group_step(pieces[0], pieces[1]), (top_all, low_all))
        low_all = jnp.roll(low_new, 1, axis=1)
    final = jnp.stack([top_all, low_all], axis=2)
    final = jnp.transpose(final, (3, 0, 1, 2, 4))
    return final.reshape(INDIV, NSNP)
```

```python
import functools

import jax
import jax.numpy as jnp
from jax import lax
from jax.experimental import pallas as pl
from jax.experimental.pallas import tpu as pltpu
from jax.sharding import PartitionSpec as P

ROUNDS = 3
SUB = 8
PANEL = 32
CHUNK = 512

epsilon = 1e-05
f32 = jnp.float32


def passed_along(array, axis, by):
    size = lax.axis_size(axis)
    return lax.ppermute(array, axis, [(i, (i + by) % size) for i in range(size)])


def standardize(counts):
    values = counts.astype(jnp.float32)
    col_mean = jnp.mean(values, axis=0)
    centred = values - col_mean
    col_var = jnp.mean(centred * centred, axis=0)
    return (centred / jnp.sqrt(col_var + epsilon)).astype(jnp.bfloat16)


def dot(a, b, ca, cb):
    return lax.dot_general(
        a, b, (((ca,), (cb,)), ((), ())), precision=lax.Precision.HIGHEST, preferred_element_type=f32
    )


def dot16(a, b, ca, cb):
    return lax.dot_general(a, b, (((ca,), (cb,)), ((), ())), preferred_element_type=f32)


def identity(size):
    rows = lax.broadcasted_iota(jnp.int32, (size, size), 0)
    cols = lax.broadcasted_iota(jnp.int32, (size, size), 1)
    return (rows == cols).astype(f32)


def inverse_of(x):
    guess = pl.reciprocal(x, approx=True)
    return guess * (2.0 - x * guess)


def panel_inverse(panel, size):
    width = 4 * size
    half = 2 * size
    tile = (SUB, width)
    first = lax.broadcasted_iota(jnp.int32, tile, 1) < half
    sub = lax.broadcasted_iota(jnp.int32, tile, 0)
    count = size // SUB
    work = [panel[SUB * t : SUB * t + SUB, :] for t in range(count)]
    done = []
    for g in range(count):
        columns = []
        for j in range(SUB):
            k = SUB * g + j
            columns.append(
                {
                    t: jnp.where(
                        first,
                        jnp.broadcast_to(work[t][:, k : k + 1], tile),
                        jnp.broadcast_to(work[t][:, half + k : half + k + 1], tile),
                    )
                    for t in range(g, count)
                }
            )
        pivots = jnp.ones(tile, f32)
        for j in range(SUB):
            pivot = jnp.broadcast_to(columns[j][g][j : j + 1, :], tile)
            pivots = jnp.where(sub == j, pivot, pivots)
            inverse = inverse_of(pivot)
            row = jnp.broadcast_to(work[g][j : j + 1, :], tile)
            heads = {m: jnp.broadcast_to(columns[m][g][j : j + 1, :], tile) for m in range(j + 1, SUB)}
            for t in range(g, count):
                factor = columns[j][t] * inverse
                if t == g:
                    factor = jnp.where(sub > j, factor, 0.0)
                for m in range(j + 1, SUB):
                    columns[m][t] = columns[m][t] - factor * heads[m]
                work[t] = work[t] - factor * row
        done.append(work[g] * lax.rsqrt(pivots))
    return jnp.concatenate(done, axis=0)


def invert_factors(grams, size):
    eye = identity(PANEL)
    for start in range(0, size, PANEL):
        stop = start + PANEL
        block = [gram[start:stop, start:stop] for gram in grams]
        inverses = panel_inverse(jnp.concatenate([block[0], eye, block[1], eye], axis=1), PANEL)
        for side, gram in enumerate(grams):
            inverse = inverses[:, (2 * side + 1) * PANEL : (2 * side + 2) * PANEL]
            rows = dot(inverse, gram[start:stop, :], 1, 0)
            gram[start:stop, :] = rows
            if stop < size:
                gram[stop:size, :] = gram[stop:size, :] - dot(rows[:, stop:size], rows, 0, 0)


def round_kernel(top_ref, low_ref, low_out, inv_out, mix_out, cross_ref, norm_ref, gram1, gram2):
    indiv, size = top_ref.shape
    cross_ref[...] = jnp.zeros_like(cross_ref)
    norm_ref[...] = jnp.zeros_like(norm_ref)

    def accumulate(step, carry):
        rows = pl.ds(step * CHUNK, CHUNK)
        top = top_ref[rows, :]
        low = low_ref[rows, :]
        cross_ref[...] += dot16(top, low, 0, 0)
        top = top.astype(f32)
        low = low.astype(f32)
        norm_ref[0:1, :] += jnp.sum(top * top, axis=0, keepdims=True)
        norm_ref[SUB : SUB + 1, :] += jnp.sum(low * low, axis=0, keepdims=True)
        return carry

    lax.fori_loop(0, indiv // CHUNK, accumulate, 0)
    norm_top = dot(norm_ref[0:SUB, :], jnp.ones((SUB, size), f32), 0, 0)
    norm_low = norm_ref[SUB : SUB + 1, :]
    coupling = 2.0 * cross_ref[...] / (norm_top + norm_low + epsilon)
    eye = identity(size)
    gram1[:, 0:size] = eye + dot(coupling, coupling, 1, 1)
    gram1[:, size : 2 * size] = eye
    gram2[:, 0:size] = eye + dot(coupling, coupling, 0, 0)
    gram2[:, size : 2 * size] = eye
    invert_factors((gram1, gram2), size)
    inverse1 = gram1[:, size : 2 * size]
    inverse2 = gram2[:, size : 2 * size]
    inv_out[...] = inverse1.astype(jnp.bfloat16)
    mix_out[...] = (-dot(inverse1, coupling, 1, 0)).astype(jnp.bfloat16)
    from_top = dot(coupling, inverse2, 1, 1).astype(jnp.bfloat16)
    from_low = inverse2.astype(jnp.bfloat16)

    def apply(step, carry):
        rows = pl.ds(step * CHUNK, CHUNK)
        low_out[rows, :] = (
            dot16(top_ref[rows, :], from_top, 1, 0) + dot16(low_ref[rows, :], from_low, 1, 1)
        ).astype(jnp.bfloat16)
        return carry

    lax.fori_loop(0, indiv // CHUNK, apply, 0)


def rotate_low(top, low):
    indiv, size = top.shape
    square = jax.ShapeDtypeStruct((size, size), jnp.bfloat16)
    return pl.pallas_call(
        round_kernel,
        out_shape=[jax.ShapeDtypeStruct((indiv, size), jnp.bfloat16), square, square],
        scratch_shapes=[
            pltpu.VMEM((size, size), f32),
            pltpu.VMEM((2 * SUB, size), f32),
            pltpu.VMEM((size, 2 * size), f32),
            pltpu.VMEM((size, 2 * size), f32),
        ],
        compiler_params=pltpu.CompilerParams(vmem_limit_bytes=40 * 2**20),
        cost_estimate=pl.CostEstimate(
            flops=4 * indiv * size * size, bytes_accessed=6 * indiv * size, transcendentals=0
        ),
        name="rotate_low",
    )(top, low)


def top_kernel(top_ref, low_ref, inv_ref, mix_ref, out_ref):
    out_ref[...] = (
        dot16(top_ref[...], inv_ref[...], 1, 1) + dot16(low_ref[...], mix_ref[...], 1, 1)
    ).astype(jnp.bfloat16)


def rotate_top(top, low, inverse, mix):
    indiv, size = top.shape
    rows = pl.BlockSpec((CHUNK, size), lambda i: (i, 0))
    whole = pl.BlockSpec((size, size), lambda i: (0, 0))
    return pl.pallas_call(
        top_kernel,
        grid=(indiv // CHUNK,),
        in_specs=[rows, rows, whole, whole],
        out_specs=rows,
        out_shape=jax.ShapeDtypeStruct((indiv, size), jnp.bfloat16),
        cost_estimate=pl.CostEstimate(
            flops=4 * indiv * size * size, bytes_accessed=6 * indiv * size, transcendentals=0
        ),
        name="rotate_top",
    )(top, low, inverse, mix)


def body(genotypes, dest_group):
    num_groups = lax.axis_size("group")
    num_pairs = lax.axis_size("pair")
    own_group = lax.axis_index("group")
    own_pair = lax.axis_index("pair")
    blk_width = genotypes.shape[1] // 2
    scaled = standardize(genotypes)
    first_block = scaled[:, :blk_width]
    second_block = scaled[:, blk_width:]
    dest_table = dest_group.reshape(num_groups, num_pairs, 2)
    column = lax.dynamic_index_in_dim(dest_table, own_pair, 1, keepdims=False)
    own_dest = lax.dynamic_index_in_dim(column, own_group, 0, keepdims=False)
    offset_zero = (own_dest[0] - own_group) % num_groups
    offset_one = (own_dest[1] - own_group) % num_groups
    top_block = jnp.where(offset_zero == 0, first_block, jnp.zeros_like(first_block))
    low_block = jnp.where(offset_one == 0, second_block, jnp.zeros_like(second_block))
    for distance in range(1, num_groups):
        outgoing = jnp.where(offset_zero == distance, first_block, second_block)
        incoming = passed_along(outgoing, "group", distance)
        top_block = jnp.where(offset_zero == distance, incoming, top_block)
        low_block = jnp.where(offset_one == distance, incoming, low_block)
    for cycle_round in range(ROUNDS):
        low_new, inverse, mix = rotate_low(top_block, low_block)
        low_next = passed_along(low_new, "pair", 1)
        top_block = rotate_top(top_block, low_block, inverse, mix)
        low_block = low_next
    return jnp.concatenate([top_block, low_block], axis=1)


def solution(mesh):
    in_specs = (P(None, ("group", "pair")), P())
    out_specs = P(None, ("group", "pair"))
    return jax.shard_map(body, mesh=mesh, in_specs=in_specs, out_specs=out_specs, check_vma=False)
```

```python
import functools

import jax
import jax.numpy as jnp
from jax import lax
from jax.experimental import pallas as pl
from jax.experimental.pallas import tpu as pltpu
from jax.sharding import PartitionSpec as P

ROUNDS = 3
SUB = 8
PANEL = 32
CHUNK = 512

epsilon = 1e-05
f32 = jnp.float32


def passed_along(array, axis, by):
    size = lax.axis_size(axis)
    return lax.ppermute(array, axis, [(i, (i + by) % size) for i in range(size)])


def dot(a, b, ca, cb):
    return lax.dot_general(
        a, b, (((ca,), (cb,)), ((), ())), precision=lax.Precision.HIGHEST, preferred_element_type=f32
    )


def dot16(a, b, ca, cb):
    return lax.dot_general(a, b, (((ca,), (cb,)), ((), ())), preferred_element_type=f32)


def identity(size):
    rows = lax.broadcasted_iota(jnp.int32, (size, size), 0)
    cols = lax.broadcasted_iota(jnp.int32, (size, size), 1)
    return (rows == cols).astype(f32)


def inverse_of(x):
    guess = pl.reciprocal(x, approx=True)
    return guess * (2.0 - x * guess)


def panel_inverse(panel, size):
    width = 4 * size
    half = 2 * size
    tile = (SUB, width)
    first = lax.broadcasted_iota(jnp.int32, tile, 1) < half
    sub = lax.broadcasted_iota(jnp.int32, tile, 0)
    count = size // SUB
    work = [panel[SUB * t : SUB * t + SUB, :] for t in range(count)]
    done = []
    for g in range(count):
        columns = []
        for j in range(SUB):
            k = SUB * g + j
            columns.append(
                {
                    t: jnp.where(
                        first,
                        jnp.broadcast_to(work[t][:, k : k + 1], tile),
                        jnp.broadcast_to(work[t][:, half + k : half + k + 1], tile),
                    )
                    for t in range(g, count)
                }
            )
        pivots = jnp.ones(tile, f32)
        for j in range(SUB):
            pivot = jnp.broadcast_to(columns[j][g][j : j + 1, :], tile)
            pivots = jnp.where(sub == j, pivot, pivots)
            inverse = inverse_of(pivot)
            row = jnp.broadcast_to(work[g][j : j + 1, :], tile)
            heads = {m: jnp.broadcast_to(columns[m][g][j : j + 1, :], tile) for m in range(j + 1, SUB)}
            for t in range(g, count):
                factor = columns[j][t] * inverse
                if t == g:
                    factor = jnp.where(sub > j, factor, 0.0)
                for m in range(j + 1, SUB):
                    columns[m][t] = columns[m][t] - factor * heads[m]
                work[t] = work[t] - factor * row
        done.append(work[g] * lax.rsqrt(pivots))
    return jnp.concatenate(done, axis=0)


def split(x):
    first = x.astype(jnp.bfloat16)
    rest = x - first.astype(f32)
    second = rest.astype(jnp.bfloat16)
    return first, second, (rest - second.astype(f32)).astype(jnp.bfloat16)


LEFT = (0, 0, 1, 0, 1, 2)
RIGHT = (0, 1, 0, 2, 1, 0)


def stacked(terms, order, axis):
    return jnp.concatenate([terms[i] for i in order], axis=axis)


def invert_factors(grams, size):
    wide = (PANEL, 4 * PANEL)
    lane = lax.broadcasted_iota(jnp.int32, wide, 1)
    sub = lax.broadcasted_iota(jnp.int32, wide, 0)
    inverse_part = lane % (2 * PANEL) >= PANEL
    eyes = (lane % (2 * PANEL) == sub + PANEL).astype(f32)
    row_lane = lax.broadcasted_iota(jnp.int32, (PANEL, size), 1)
    row_sub = lax.broadcasted_iota(jnp.int32, (PANEL, size), 0)
    all_lane = lax.broadcasted_iota(jnp.int32, (size, size), 1)
    zero = jnp.zeros((PANEL, size), f32)

    def step(index, carry):
        start = pl.multiple_of(index * PANEL, PANEL)
        stop = start + PANEL
        rows = [gram[pl.ds(start, PANEL), :] for gram in grams]
        blocks = []
        for side in range(2):
            block = rows[side][:, 0 : 4 * PANEL]
            for at in range(4 * PANEL, size, 4 * PANEL):
                block = jnp.where(start >= at, rows[side][:, at : at + 4 * PANEL], block)
            blocks.append(pltpu.roll(block, lax.rem(2 * PANEL * side + 4 * size - start, 4 * PANEL), 1))
        panel = jnp.where(inverse_part, eyes, jnp.where(lane < 2 * PANEL, blocks[0], blocks[1]))
        inverse = jnp.where(inverse_part, panel_inverse(panel, PANEL), 0.0)
        inverse = jnp.concatenate(
            [jnp.where(lane < 2 * PANEL, inverse, 0.0), jnp.where(lane >= 2 * PANEL, inverse, 0.0)], axis=0
        )
        within = (row_lane >= start) & (row_lane < stop)
        eye = (row_lane - start == row_sub).astype(f32)
        rows = [jnp.where(within, eye, part) for part in rows]
        left = split(inverse)
        right = split(jnp.concatenate([zero, rows[0], zero, rows[1]], axis=0))
        done = dot16(stacked(left, LEFT, 1), stacked(right, RIGHT, 0), 1, 0)
        terms = split(done)
        for side, gram in enumerate(grams):
            own = slice(side * PANEL, (side + 1) * PANEL)
            right = [term[own, :] for term in terms]
            left = [jnp.where(row_lane >= stop, term, jnp.zeros_like(term)) for term in right]
            change = dot16(stacked(left, LEFT, 0), stacked(right, RIGHT, 0), 0, 0)
            gram[...] = jnp.where((all_lane >= start) & (all_lane < stop), 0.0, gram[...]) - change
            gram[pl.ds(start, PANEL), :] = done[own, :]
        return carry

    lax.fori_loop(0, size // PANEL, step, 0)


def take_grams(rows, top_ref, low_ref, cross_ref, norm_ref):
    top = top_ref[rows, :]
    low = low_ref[rows, :]
    cross_ref[...] += dot16(top, low, 0, 0)
    top = top.astype(f32)
    low = low.astype(f32)
    norm_ref[0:1, :] += jnp.sum(top * top, axis=0, keepdims=True)
    norm_ref[SUB : SUB + 1, :] += jnp.sum(low * low, axis=0, keepdims=True)


def rotate(refs, outs, scratch, sems):
    top_ref, low_ref = refs
    low_out, inv_out, mix_out = outs
    cross_ref, norm_ref, gram1, gram2, new_ref, inv_ref, mix_ref = scratch
    indiv, size = top_ref.shape
    norm_top = dot(norm_ref[0:SUB, :], jnp.ones((SUB, size), f32), 0, 0)
    norm_low = norm_ref[SUB : SUB + 1, :]
    coupling = 2.0 * cross_ref[...] / (norm_top + norm_low + epsilon)
    eye = identity(size)
    gram1[...] = eye + dot(coupling, coupling, 1, 1)
    gram2[...] = eye + dot(coupling, coupling, 0, 0)
    invert_factors((gram1, gram2), size)
    below = lax.broadcasted_iota(jnp.int32, (size, size), 0) >= lax.broadcasted_iota(jnp.int32, (size, size), 1)
    inverse1 = jnp.where(below, gram1[...], 0.0)
    inverse2 = jnp.where(below, gram2[...], 0.0)
    from_top = dot(coupling, inverse2, 1, 1).astype(jnp.bfloat16)
    from_low = inverse2.astype(jnp.bfloat16)
    count = indiv // CHUNK

    def sent(step):
        rows = pl.ds(pl.multiple_of(step * CHUNK, CHUNK), CHUNK)
        return pltpu.make_async_copy(new_ref.at[rows, :], low_out.at[rows, :], sems.at[step])

    def apply(step, carry):
        rows = pl.ds(pl.multiple_of(step * CHUNK, CHUNK), CHUNK)
        new_ref[rows, :] = (
            dot16(top_ref[rows, :], from_top, 1, 0) + dot16(low_ref[rows, :], from_low, 1, 1)
        ).astype(jnp.bfloat16)
        sent(step).start()
        return carry

    lax.fori_loop(0, count, apply, 0)
    inv_ref[...] = inverse1.astype(jnp.bfloat16)
    mix_ref[...] = (-dot(inverse1, coupling, 1, 0)).astype(jnp.bfloat16)
    small = [
        pltpu.make_async_copy(inv_ref, inv_out, sems.at[count]),
        pltpu.make_async_copy(mix_ref, mix_out, sems.at[count + 1]),
    ]
    for copy in small:
        copy.start()
    for step in range(count):
        sent(step).wait()
    for copy in small:
        copy.wait()


def scratch_of(indiv, size):
    block = pltpu.VMEM((indiv, size), jnp.bfloat16)
    small = pltpu.VMEM((size, size), jnp.bfloat16)
    count = indiv // CHUNK
    return [
        block,
        block,
        pltpu.VMEM((size, size), f32),
        pltpu.VMEM((2 * SUB, size), f32),
        pltpu.VMEM((size, size), f32),
        pltpu.VMEM((size, size), f32),
        block,
        small,
        small,
        pltpu.SemaphoreType.DMA((count + 2,)),
        pltpu.SemaphoreType.DMA((2 * count,)),
    ]


def cost(indiv, size):
    return pl.CostEstimate(flops=40 * indiv * size * size, bytes_accessed=16 * indiv * size, transcendentals=0)


def round_kernel(top_hbm, low_hbm, low_out, inv_out, mix_out, top_ref, low_ref, cross_ref, norm_ref, *rest):
    *scratch, sems, in_sems = rest
    indiv, size = top_ref.shape
    count = indiv // CHUNK

    def fetched(step):
        rows = pl.ds(pl.multiple_of(step * CHUNK, CHUNK), CHUNK)
        return [
            pltpu.make_async_copy(top_hbm.at[rows, :], top_ref.at[rows, :], in_sems.at[2 * step]),
            pltpu.make_async_copy(low_hbm.at[rows, :], low_ref.at[rows, :], in_sems.at[2 * step + 1]),
        ]

    for step in range(count):
        for copy in fetched(step):
            copy.start()
    cross_ref[...] = jnp.zeros_like(cross_ref)
    norm_ref[...] = jnp.zeros_like(norm_ref)

    def accumulate(step, carry):
        for copy in fetched(step):
            copy.wait()
        take_grams(pl.ds(pl.multiple_of(step * CHUNK, CHUNK), CHUNK), top_ref, low_ref, cross_ref, norm_ref)
        return carry

    lax.fori_loop(0, count, accumulate, 0)
    rotate((top_ref, low_ref), (low_out, inv_out, mix_out), (cross_ref, norm_ref, *scratch), sems)


def rotate_low(top, low):
    indiv, size = top.shape
    square = jax.ShapeDtypeStruct((size, size), jnp.bfloat16)
    anywhere = pl.BlockSpec(memory_space=pl.ANY)
    return pl.pallas_call(
        round_kernel,
        in_specs=[anywhere] * 2,
        out_specs=[anywhere] * 3,
        out_shape=[jax.ShapeDtypeStruct((indiv, size), jnp.bfloat16), square, square],
        scratch_shapes=scratch_of(indiv, size),
        compiler_params=pltpu.CompilerParams(vmem_limit_bytes=16 * 2**20),
        cost_estimate=cost(indiv, size),
        name="rotate_low",
    )(top, low)


def first_kernel(slots, flags, *refs):
    inputs = 6 if slots == 2 else 13
    sources = refs[:6] if slots == 2 else refs[:8]
    low_out, inv_out, mix_out, top_scaled, low_scaled = refs[inputs : inputs + 5]
    top_ref, low_ref, cross_ref, norm_ref, *rest = refs[inputs + 5 :]
    *scratch, sems, in_sems = rest
    own, other = sources[0:2], sources[2:4]
    indiv, size = top_ref.shape
    half = indiv // 2
    count = indiv // CHUNK
    core = flags[3]

    @pl.when(flags[0] == 1)
    def _():
        def fetch(code, target, parts, side):
            for part in range(2):
                place = jnp.where(core == part, 0, half)
                place = pl.multiple_of(place, half)

                @pl.when(flags[1 + side] == code)
                def _():
                    pltpu.make_async_copy(
                        parts[part], target.at[pl.ds(place, half), :], in_sems.at[2 * side + part]
                    ).start()

        for side, target in enumerate((top_ref, low_ref)):
            columns = slice(side * size, (side + 1) * size)
            choices = [[ref.at[:, columns] for ref in own], [ref.at[:, columns] for ref in other]]
            for slot in range(2):
                columns = slice(slot * size, (slot + 1) * size)
                choices.append([ref.at[:, columns] for ref in sources[4:6]])
            if slots == 3:
                choices.append(list(sources[6:8]))
            for code, parts in enumerate(choices):
                fetch(code, target, parts, side)
        cross_ref[...] = jnp.zeros_like(cross_ref)
        norm_ref[...] = jnp.zeros_like(norm_ref)
        scales = []
        for side, target in enumerate((top_ref, low_ref)):
            for part in range(2):
                pltpu.make_async_copy(
                    own[0].at[:, 0:size], target.at[pl.ds(0, half), :], in_sems.at[2 * side + part]
                ).wait()

            def add(step, sums):
                values = target[pl.ds(pl.multiple_of(step * CHUNK, CHUNK), CHUNK), :].astype(f32)
                return (
                    sums[0] + jnp.sum(values, axis=0, keepdims=True),
                    sums[1] + jnp.sum(values * values, axis=0, keepdims=True),
                )

            total, squares = lax.fori_loop(0, count, add, (jnp.zeros((1, size), f32),) * 2)
            whole = total.astype(jnp.int32)
            spread = indiv * squares.astype(jnp.int32) - whole * whole
            variance = spread.astype(f32) * (1.0 / (indiv * indiv))
            scales.append((total * (1.0 / indiv), 1.0 / jnp.sqrt(variance + epsilon)))

        def kept(step):
            rows = pl.ds(pl.multiple_of(step * CHUNK, CHUNK), CHUNK)
            return [
                pltpu.make_async_copy(target.at[rows, :], scaled.at[rows, :], in_sems.at[4 + 2 * step + side])
                for side, (target, scaled) in enumerate(((top_ref, top_scaled), (low_ref, low_scaled)))
            ]

        def scale_rows(step, carry):
            rows = pl.ds(pl.multiple_of(step * CHUNK, CHUNK), CHUNK)
            for (mean, scale), target in zip(scales, (top_ref, low_ref)):
                target[rows, :] = ((target[rows, :].astype(f32) - mean) * scale).astype(jnp.bfloat16)
            for copy in kept(step):
                copy.start()
            take_grams(rows, top_ref, low_ref, cross_ref, norm_ref)
            return carry

        lax.fori_loop(0, count, scale_rows, 0)
        rotate((top_ref, low_ref), (low_out, inv_out, mix_out), (cross_ref, norm_ref, *scratch), sems)
        for step in range(count):
            for copy in kept(step):
                copy.wait()


def first_round(flags, sources, held=()):
    half, size = sources[0].shape[0], sources[0].shape[1] // 2
    indiv = 2 * half
    slots = 3 if held else 2
    block = jax.ShapeDtypeStruct((indiv, size), jnp.bfloat16)
    square = jax.ShapeDtypeStruct((size, size), jnp.bfloat16)
    anywhere = pl.BlockSpec(memory_space=pl.ANY)
    scratch = scratch_of(indiv, size)
    scratch[-1] = pltpu.SemaphoreType.DMA((2 * (indiv // CHUNK) + 4,))
    return pl.pallas_call(
        functools.partial(first_kernel, slots),
        in_specs=[pl.BlockSpec(memory_space=pltpu.SMEM)] + [anywhere] * (len(sources) + len(held)),
        out_specs=[anywhere] * 5,
        out_shape=[block, square, square, block, block],
        input_output_aliases={1 + len(sources) + i: i for i in range(len(held))},
        scratch_shapes=scratch,
        compiler_params=pltpu.CompilerParams(vmem_limit_bytes=16 * 2**20),
        cost_estimate=cost(indiv, size),
        name="first_round",
    )(flags, *sources, *held)


def top_kernel(top_ref, low_ref, inv_ref, mix_ref, out_ref):
    out_ref[...] = (
        dot16(top_ref[...], inv_ref[...], 1, 1) + dot16(low_ref[...], mix_ref[...], 1, 1)
    ).astype(jnp.bfloat16)


def rotate_top(top, low, inverse, mix, blocks=1):
    indiv, size = top.shape
    rows = pl.BlockSpec((CHUNK, size), lambda i: (i, 0))
    whole = pl.BlockSpec((size, size), lambda i: (0, 0))
    return pl.pallas_call(
        top_kernel,
        grid=(indiv // CHUNK,),
        in_specs=[rows, rows, whole, whole],
        out_specs=rows,
        out_shape=jax.ShapeDtypeStruct((indiv, blocks * size), jnp.bfloat16),
        cost_estimate=pl.CostEstimate(
            flops=4 * indiv * size * size, bytes_accessed=6 * indiv * size, transcendentals=0
        ),
        name="rotate_top",
    )(top, low, inverse, mix)


def place_kernel(low_ref, held_ref, out_ref):
    out_ref[...] = low_ref[...]


def place_low(low, held):
    indiv, size = low.shape
    return pl.pallas_call(
        place_kernel,
        grid=(indiv // CHUNK,),
        in_specs=[pl.BlockSpec((CHUNK, size), lambda i: (i, 0)), pl.BlockSpec(memory_space=pl.ANY)],
        out_specs=pl.BlockSpec((CHUNK, size), lambda i: (i, 1)),
        out_shape=jax.ShapeDtypeStruct(held.shape, held.dtype),
        input_output_aliases={1: 0},
        name="place_low",
    )(low, held)


def across(array, bit):
    size = lax.axis_size("group")
    return lax.ppermute(array, "group", [(i, i ^ bit) for i in range(size)])


def regrouped_first_round(genotypes, dest_group):
    num_groups = lax.axis_size("group")
    num_pairs = lax.axis_size("pair")
    own_pair = lax.axis_index("pair")
    core = lax.axis_index("group") % 2
    size = genotypes.shape[1] // 2
    half = genotypes.shape[0] // 2
    offsets = lax.dynamic_index_in_dim(
        dest_group.reshape(num_groups, num_pairs, 2)[0], own_pair, 0, keepdims=False
    )
    crossing = [[(offsets[k] == 1 + c) | (offsets[k] == 2 + c) for k in range(2)] for c in range(2)]
    slot = [[None, None], [None, None]]
    used = jnp.int32(0)
    side_of = [jnp.int32(0)] * 3
    core_of = [jnp.int32(0)] * 3
    for c in range(2):
        for k in range(2):
            slot[c][k] = used
            for i in range(3):
                here = crossing[c][k] & (used == i)
                side_of[i] = jnp.where(here, k, side_of[i])
                core_of[i] = jnp.where(here, (offsets[k] + c) % 2, core_of[i])
            used = used + crossing[c][k].astype(jnp.int32)
    codes = []
    for k in range(2):
        far = jnp.where(core == 0, crossing[0][k], crossing[1][k])
        place = 2 + jnp.where(core == 0, slot[0][k], slot[1][k])
        codes.append(jnp.where(far, place, jnp.where(offsets[k] == 0, 0, 1)))

    def counts(which):
        rows = lax.dynamic_slice_in_dim(genotypes, which * half, half, 0)
        return rows.astype(jnp.bfloat16)

    own_away = counts(1 - core)
    other_here = across(own_away, 1)
    own_here = counts(core)

    def payload(i):
        near = lax.dynamic_slice_in_dim(own_here, side_of[i] * size, size, 1)
        far = lax.dynamic_slice_in_dim(other_here, side_of[i] * size, size, 1)
        return jnp.where(core_of[i] == core, near, far)

    early = across(jnp.concatenate([payload(0), payload(1)], axis=1), 2)
    other_away = across(own_here, 1)
    late, early = lax.optimization_barrier((payload(2), early))
    late = across(late, 2)
    early_away = across(early, 1)
    sources = (own_here, own_away, other_here, other_away, early, early_away)

    def flags(which):
        return jnp.stack([(core == which).astype(jnp.int32), codes[0], codes[1], core]).astype(jnp.int32)

    held = list(first_round(flags(0), sources))
    late, held[1] = lax.optimization_barrier((late, held[1]))
    late_away = across(late, 1)
    return first_round(flags(1), sources + (late, late_away), tuple(held))


def body(genotypes, dest_group):
    low_new, inverse, mix, top, low = regrouped_first_round(genotypes, dest_group)
    for cycle_round in range(1, ROUNDS):
        low_next = passed_along(low_new, "pair", 1)
        top = rotate_top(top, low, inverse, mix)
        low = low_next
        low_new, inverse, mix = rotate_low(top, low)
    low_next = passed_along(low_new, "pair", 1)
    return place_low(low_next, rotate_top(top, low, inverse, mix, 2))


def solution(mesh):
    in_specs = (P(None, ("group", "pair")), P())
    out_specs = P(None, ("group", "pair"))
    return jax.shard_map(body, mesh=mesh, in_specs=in_specs, out_specs=out_specs, check_vma=False)
```

```python
import functools

import jax
import jax.numpy as jnp
from jax import lax
from jax.experimental import pallas as pl
from jax.experimental.pallas import tpu as pltpu
from jax.sharding import PartitionSpec as P

ROUNDS = 3
SUB = 8
PANEL = 32
CHUNK = 512

epsilon = 1e-05
f32 = jnp.float32


def passed_along(array, axis, by):
    size = lax.axis_size(axis)
    return lax.ppermute(array, axis, [(i, (i + by) % size) for i in range(size)])


def dot(a, b, ca, cb):
    return lax.dot_general(
        a, b, (((ca,), (cb,)), ((), ())), precision=lax.Precision.HIGHEST, preferred_element_type=f32
    )


def dot16(a, b, ca, cb):
    return lax.dot_general(a, b, (((ca,), (cb,)), ((), ())), preferred_element_type=f32)


def identity(size):
    rows = lax.broadcasted_iota(jnp.int32, (size, size), 0)
    cols = lax.broadcasted_iota(jnp.int32, (size, size), 1)
    return (rows == cols).astype(f32)


def inverse_of(x):
    guess = pl.reciprocal(x, approx=True)
    return guess * (2.0 - x * guess)


def panel_inverse(panel, size):
    width = 4 * size
    half = 2 * size
    tile = (SUB, width)
    first = lax.broadcasted_iota(jnp.int32, tile, 1) < half
    sub = lax.broadcasted_iota(jnp.int32, tile, 0)
    count = size // SUB
    work = [panel[SUB * t : SUB * t + SUB, :] for t in range(count)]
    done = []
    for g in range(count):
        columns = []
        for j in range(SUB):
            k = SUB * g + j
            columns.append(
                {
                    t: jnp.where(
                        first,
                        jnp.broadcast_to(work[t][:, k : k + 1], tile),
                        jnp.broadcast_to(work[t][:, half + k : half + k + 1], tile),
                    )
                    for t in range(g, count)
                }
            )
        pivots = jnp.ones(tile, f32)
        for j in range(SUB):
            pivot = jnp.broadcast_to(columns[j][g][j : j + 1, :], tile)
            pivots = jnp.where(sub == j, pivot, pivots)
            inverse = inverse_of(pivot)
            row = jnp.broadcast_to(work[g][j : j + 1, :], tile)
            heads = {m: jnp.broadcast_to(columns[m][g][j : j + 1, :], tile) for m in range(j + 1, SUB)}
            for t in range(g, count):
                factor = columns[j][t] * inverse
                if t == g:
                    factor = jnp.where(sub > j, factor, 0.0)
                for m in range(j + 1, SUB):
                    columns[m][t] = columns[m][t] - factor * heads[m]
                work[t] = work[t] - factor * row
        done.append(work[g] * lax.rsqrt(pivots))
    return jnp.concatenate(done, axis=0)


def split(x):
    first = x.astype(jnp.bfloat16)
    rest = x - first.astype(f32)
    second = rest.astype(jnp.bfloat16)
    return first, second, (rest - second.astype(f32)).astype(jnp.bfloat16)


LEFT = (0, 0, 1, 0, 1, 2)
RIGHT = (0, 1, 0, 2, 1, 0)


def stacked(terms, order, axis):
    return jnp.concatenate([terms[i] for i in order], axis=axis)


def invert_factors(grams, size):
    wide = (PANEL, 4 * PANEL)
    lane = lax.broadcasted_iota(jnp.int32, wide, 1)
    sub = lax.broadcasted_iota(jnp.int32, wide, 0)
    inverse_part = lane % (2 * PANEL) >= PANEL
    eyes = (lane % (2 * PANEL) == sub + PANEL).astype(f32)
    row_lane = lax.broadcasted_iota(jnp.int32, (PANEL, size), 1)
    row_sub = lax.broadcasted_iota(jnp.int32, (PANEL, size), 0)
    all_lane = lax.broadcasted_iota(jnp.int32, (size, size), 1)
    zero = jnp.zeros((PANEL, size), f32)

    def step(index, carry):
        start = pl.multiple_of(index * PANEL, PANEL)
        stop = start + PANEL
        rows = [gram[pl.ds(start, PANEL), :] for gram in grams]
        blocks = []
        for side in range(2):
            block = rows[side][:, 0 : 4 * PANEL]
            for at in range(4 * PANEL, size, 4 * PANEL):
                block = jnp.where(start >= at, rows[side][:, at : at + 4 * PANEL], block)
            blocks.append(pltpu.roll(block, lax.rem(2 * PANEL * side + 4 * size - start, 4 * PANEL), 1))
        panel = jnp.where(inverse_part, eyes, jnp.where(lane < 2 * PANEL, blocks[0], blocks[1]))
        inverse = jnp.where(inverse_part, panel_inverse(panel, PANEL), 0.0)
        inverse = jnp.concatenate(
            [jnp.where(lane < 2 * PANEL, inverse, 0.0), jnp.where(lane >= 2 * PANEL, inverse, 0.0)], axis=0
        )
        within = (row_lane >= start) & (row_lane < stop)
        eye = (row_lane - start == row_sub).astype(f32)
        rows = [jnp.where(within, eye, part) for part in rows]
        left = split(inverse)
        right = split(jnp.concatenate([zero, rows[0], zero, rows[1]], axis=0))
        done = dot16(stacked(left, LEFT, 1), stacked(right, RIGHT, 0), 1, 0)
        terms = split(done)
        for side, gram in enumerate(grams):
            own = slice(side * PANEL, (side + 1) * PANEL)
            right = [term[own, :] for term in terms]
            left = [jnp.where(row_lane >= stop, term, jnp.zeros_like(term)) for term in right]
            change = dot16(stacked(left, LEFT, 0), stacked(right, RIGHT, 0), 0, 0)
            gram[...] = jnp.where((all_lane >= start) & (all_lane < stop), 0.0, gram[...]) - change
            gram[pl.ds(start, PANEL), :] = done[own, :]
        return carry

    lax.fori_loop(0, size // PANEL, step, 0)


def take_grams(rows, top_ref, low_ref, cross_ref, norm_ref):
    top = top_ref[rows, :]
    low = low_ref[rows, :]
    cross_ref[...] += dot16(top, low, 0, 0)
    top = top.astype(f32)
    low = low.astype(f32)
    norm_ref[0:1, :] += jnp.sum(top * top, axis=0, keepdims=True)
    norm_ref[SUB : SUB + 1, :] += jnp.sum(low * low, axis=0, keepdims=True)


def rotate(refs, outs, scratch, sems):
    top_ref, low_ref = refs
    low_out, inv_out, mix_out = outs
    cross_ref, norm_ref, gram1, gram2, new_ref, inv_ref, mix_ref = scratch
    indiv, size = top_ref.shape
    norm_top = dot(norm_ref[0:SUB, :], jnp.ones((SUB, size), f32), 0, 0)
    norm_low = norm_ref[SUB : SUB + 1, :]
    coupling = 2.0 * cross_ref[...] / (norm_top + norm_low + epsilon)
    eye = identity(size)
    gram1[...] = eye + dot(coupling, coupling, 1, 1)
    gram2[...] = eye + dot(coupling, coupling, 0, 0)
    invert_factors((gram1, gram2), size)
    below = lax.broadcasted_iota(jnp.int32, (size, size), 0) >= lax.broadcasted_iota(jnp.int32, (size, size), 1)
    inverse1 = jnp.where(below, gram1[...], 0.0)
    inverse2 = jnp.where(below, gram2[...], 0.0)
    from_top = dot(coupling, inverse2, 1, 1).astype(jnp.bfloat16)
    from_low = inverse2.astype(jnp.bfloat16)
    count = indiv // CHUNK

    def sent(step):
        rows = pl.ds(pl.multiple_of(step * CHUNK, CHUNK), CHUNK)
        return pltpu.make_async_copy(new_ref.at[rows, :], low_out.at[rows, :], sems.at[step])

    def apply(step, carry):
        rows = pl.ds(pl.multiple_of(step * CHUNK, CHUNK), CHUNK)
        new_ref[rows, :] = (
            dot16(top_ref[rows, :], from_top, 1, 0) + dot16(low_ref[rows, :], from_low, 1, 1)
        ).astype(jnp.bfloat16)
        sent(step).start()
        return carry

    lax.fori_loop(0, count, apply, 0)
    inv_ref[...] = inverse1.astype(jnp.bfloat16)
    mix_ref[...] = (-dot(inverse1, coupling, 1, 0)).astype(jnp.bfloat16)
    small = [
        pltpu.make_async_copy(inv_ref, inv_out, sems.at[count]),
        pltpu.make_async_copy(mix_ref, mix_out, sems.at[count + 1]),
    ]
    for copy in small:
        copy.start()
    for step in range(count):
        sent(step).wait()
    for copy in small:
        copy.wait()


def scratch_of(indiv, size):
    block = pltpu.VMEM((indiv, size), jnp.bfloat16)
    small = pltpu.VMEM((size, size), jnp.bfloat16)
    count = indiv // CHUNK
    return [
        block,
        block,
        pltpu.VMEM((size, size), f32),
        pltpu.VMEM((2 * SUB, size), f32),
        pltpu.VMEM((size, size), f32),
        pltpu.VMEM((size, size), f32),
        block,
        small,
        small,
        pltpu.SemaphoreType.DMA((count + 2,)),
        pltpu.SemaphoreType.DMA((2 * count,)),
    ]


def cost(indiv, size):
    return pl.CostEstimate(flops=40 * indiv * size * size, bytes_accessed=16 * indiv * size, transcendentals=0)


def round_kernel(top_hbm, low_hbm, low_out, inv_out, mix_out, top_ref, low_ref, cross_ref, norm_ref, *rest):
    *scratch, sems, in_sems = rest
    indiv, size = top_ref.shape
    count = indiv // CHUNK

    def fetched(step):
        rows = pl.ds(pl.multiple_of(step * CHUNK, CHUNK), CHUNK)
        return [
            pltpu.make_async_copy(top_hbm.at[rows, :], top_ref.at[rows, :], in_sems.at[2 * step]),
            pltpu.make_async_copy(low_hbm.at[rows, :], low_ref.at[rows, :], in_sems.at[2 * step + 1]),
        ]

    for step in range(count):
        for copy in fetched(step):
            copy.start()
    cross_ref[...] = jnp.zeros_like(cross_ref)
    norm_ref[...] = jnp.zeros_like(norm_ref)

    def accumulate(step, carry):
        for copy in fetched(step):
            copy.wait()
        take_grams(pl.ds(pl.multiple_of(step * CHUNK, CHUNK), CHUNK), top_ref, low_ref, cross_ref, norm_ref)
        return carry

    lax.fori_loop(0, count, accumulate, 0)
    rotate((top_ref, low_ref), (low_out, inv_out, mix_out), (cross_ref, norm_ref, *scratch), sems)


def rotate_low(top, low):
    indiv, size = top.shape
    square = jax.ShapeDtypeStruct((size, size), jnp.bfloat16)
    anywhere = pl.BlockSpec(memory_space=pl.ANY)
    return pl.pallas_call(
        round_kernel,
        in_specs=[anywhere] * 2,
        out_specs=[anywhere] * 3,
        out_shape=[jax.ShapeDtypeStruct((indiv, size), jnp.bfloat16), square, square],
        scratch_shapes=scratch_of(indiv, size),
        compiler_params=pltpu.CompilerParams(vmem_limit_bytes=16 * 2**20),
        cost_estimate=cost(indiv, size),
        name="rotate_low",
    )(top, low)


def offsets_of(dest):
    pair = lax.axis_index("pair")
    return dest[2 * pair], dest[2 * pair + 1]


def present(offsets, value):
    return (offsets[0] == value) | (offsets[1] == value)


def side_with(offsets, value):
    return jnp.where(offsets[1] == value, 1, 0)


def cast_kernel(dest, *refs):
    count = len(refs) // 2
    for counts_ref, out_ref in zip(refs[:count], refs[count:]):
        out_ref[...] = counts_ref[...].astype(out_ref.dtype)


def picked(genotypes, dest, wants):
    indiv, size = genotypes.shape[0], genotypes.shape[1] // 2
    steps = 4
    in_specs, out_specs, shapes = [], [], []
    for want in wants:
        parts = len(want((0, 0)))
        rows = indiv // steps // parts

        def place(i, dest, want=want):
            offsets = offsets_of(dest)
            value, *part = want(offsets)
            return (i + (part[0] * steps if part else 0), side_with(offsets, value))

        in_specs.append(pl.BlockSpec((rows, size), place))
        out_specs.append(pl.BlockSpec((rows, size), lambda i, dest: (i, 0)))
        shapes.append(jax.ShapeDtypeStruct((indiv // parts, size), jnp.bfloat16))
    return pl.pallas_call(
        cast_kernel,
        grid_spec=pltpu.PrefetchScalarGridSpec(
            num_scalar_prefetch=1, grid=(steps,), in_specs=in_specs, out_specs=out_specs
        ),
        out_shape=shapes,
        name="pick_blocks",
    )(dest, *[genotypes] * len(wants))


def first_kernel(wholes, halves, dest, *refs):
    sources = refs[: wholes + halves]
    held = 5 if halves else 0
    low_out, inv_out, mix_out, top_scaled, low_scaled = refs[wholes + halves + held : wholes + halves + held + 5]
    top_ref, low_ref, cross_ref, norm_ref, *rest = refs[wholes + halves + held + 5 :]
    *scratch, sems, in_sems = rest
    indiv, size = top_ref.shape
    half = indiv // 2
    count = indiv // CHUNK

    offsets = offsets_of(dest)
    if halves:
        two = jnp.where(present(offsets, 1), wholes, 2)
        codes = (0, 1, two, jnp.where(present(offsets, 2), wholes, 2))
    else:
        codes = (0, 2, 3, 1)

    @pl.when(lax.axis_index("group") % 2 == (1 if halves else 0))
    def _():
        for side, target in enumerate((top_ref, low_ref)):
            chosen = jnp.int32(codes[0])
            for offset in range(1, 4):
                chosen = jnp.where(offsets[side] == offset, codes[offset], chosen)
            for code in range(wholes + halves // 2):
                for part in range(2):
                    rows = pl.ds(part * half, half)
                    source = sources[code].at[rows, :] if code < wholes else sources[wholes + part]

                    @pl.when(chosen == code)
                    def _():
                        pltpu.make_async_copy(source, target.at[rows, :], in_sems.at[2 * side + part]).start()

        cross_ref[...] = jnp.zeros_like(cross_ref)
        norm_ref[...] = jnp.zeros_like(norm_ref)
        scales = []
        for side, target in enumerate((top_ref, low_ref)):
            for part in range(2):
                rows = pl.ds(part * half, half)
                pltpu.make_async_copy(sources[0].at[rows, :], target.at[rows, :], in_sems.at[2 * side + part]).wait()

            def add(step, sums):
                values = target[pl.ds(pl.multiple_of(step * CHUNK, CHUNK), CHUNK), :].astype(f32)
                return (
                    sums[0] + jnp.sum(values, axis=0, keepdims=True),
                    sums[1] + jnp.sum(values * values, axis=0, keepdims=True),
                )

            total, squares = lax.fori_loop(0, count, add, (jnp.zeros((1, size), f32),) * 2)
            whole = total.astype(jnp.int32)
            spread = indiv * squares.astype(jnp.int32) - whole * whole
            variance = spread.astype(f32) * (1.0 / (indiv * indiv))
            scales.append((total * (1.0 / indiv), 1.0 / jnp.sqrt(variance + epsilon)))

        def kept(step):
            rows = pl.ds(pl.multiple_of(step * CHUNK, CHUNK), CHUNK)
            return [
                pltpu.make_async_copy(target.at[rows, :], scaled.at[rows, :], in_sems.at[4 + 2 * step + side])
                for side, (target, scaled) in enumerate(((top_ref, top_scaled), (low_ref, low_scaled)))
            ]

        def scale_rows(step, carry):
            rows = pl.ds(pl.multiple_of(step * CHUNK, CHUNK), CHUNK)
            for (mean, scale), target in zip(scales, (top_ref, low_ref)):
                target[rows, :] = ((target[rows, :].astype(f32) - mean) * scale).astype(jnp.bfloat16)
            for copy in kept(step):
                copy.start()
            take_grams(rows, top_ref, low_ref, cross_ref, norm_ref)
            return carry

        lax.fori_loop(0, count, scale_rows, 0)
        rotate((top_ref, low_ref), (low_out, inv_out, mix_out), (cross_ref, norm_ref, *scratch), sems)
        for step in range(count):
            for copy in kept(step):
                copy.wait()


def first_round(dest, wholes, halves=(), held=()):
    indiv, size = wholes[0].shape
    sources = tuple(wholes) + tuple(halves)
    block = jax.ShapeDtypeStruct((indiv, size), jnp.bfloat16)
    square = jax.ShapeDtypeStruct((size, size), jnp.bfloat16)
    anywhere = pl.BlockSpec(memory_space=pl.ANY)
    scratch = scratch_of(indiv, size)
    scratch[-1] = pltpu.SemaphoreType.DMA((2 * (indiv // CHUNK) + 4,))
    return pl.pallas_call(
        functools.partial(first_kernel, len(wholes), len(halves)),
        in_specs=[pl.BlockSpec(memory_space=pltpu.SMEM)] + [anywhere] * (len(sources) + len(held)),
        out_specs=[anywhere] * 5,
        out_shape=[block, square, square, block, block],
        input_output_aliases={1 + len(sources) + i: i for i in range(len(held))},
        scratch_shapes=scratch,
        compiler_params=pltpu.CompilerParams(vmem_limit_bytes=16 * 2**20),
        cost_estimate=cost(indiv, size),
        name="first_round",
    )(dest, *sources, *held)


def top_kernel(top_ref, low_ref, inv_ref, mix_ref, out_ref):
    out_ref[...] = (
        dot16(top_ref[...], inv_ref[...], 1, 1) + dot16(low_ref[...], mix_ref[...], 1, 1)
    ).astype(jnp.bfloat16)


def rotate_top(top, low, inverse, mix, blocks=1):
    indiv, size = top.shape
    rows = pl.BlockSpec((CHUNK, size), lambda i: (i, 0))
    whole = pl.BlockSpec((size, size), lambda i: (0, 0))
    return pl.pallas_call(
        top_kernel,
        grid=(indiv // CHUNK,),
        in_specs=[rows, rows, whole, whole],
        out_specs=rows,
        out_shape=jax.ShapeDtypeStruct((indiv, blocks * size), jnp.bfloat16),
        cost_estimate=pl.CostEstimate(
            flops=4 * indiv * size * size, bytes_accessed=6 * indiv * size, transcendentals=0
        ),
        name="rotate_top",
    )(top, low, inverse, mix)


def place_kernel(low_ref, held_ref, out_ref, sem):
    size = low_ref.shape[1]
    copy = pltpu.make_async_copy(low_ref, out_ref.at[:, size : 2 * size], sem)
    copy.start()
    copy.wait()


def place_low(low, held):
    anywhere = pl.BlockSpec(memory_space=pl.ANY)
    return pl.pallas_call(
        place_kernel,
        in_specs=[pl.BlockSpec(memory_space=pltpu.VMEM), anywhere],
        out_specs=anywhere,
        out_shape=jax.ShapeDtypeStruct(held.shape, held.dtype),
        input_output_aliases={1: 0},
        scratch_shapes=[pltpu.SemaphoreType.DMA],
        name="place_low",
    )(low, held)


def regrouped_first_round(genotypes, dest_group):
    num_groups = lax.axis_size("group")
    core = lax.axis_index("group") % 2
    offsets = offsets_of(dest_group)

    def by_core(zero, one):
        return jnp.where(lax.axis_index("group") % 2 == 0, zero, one)

    def sent(array, hops):
        return lax.ppermute(array, "group", [hop for chip in range(0, num_groups, 2) for hop in hops(chip)])

    def far(chip):
        return (chip + 2) % num_groups

    (cross,) = picked(
        genotypes,
        dest_group,
        [lambda o: (by_core(jnp.where(present(o, 2), 2, 3), jnp.where(present(o, 1), 1, 2)),)],
    )
    cross_one = sent(cross, lambda chip: [(chip + 1, far(chip))])
    cross_zero = sent(cross, lambda chip: [(chip, far(chip))])
    table, _ = lax.optimization_barrier((genotypes, cross))
    near, own, lent, kept = picked(
        table,
        dest_group,
        [
            lambda o: (by_core(1, 3),),
            lambda o: (0,),
            lambda o: (by_core(3, 2), by_core(1, 0)),
            lambda o: (by_core(3, 2), by_core(0, 1)),
        ],
    )
    lent = sent(lent, lambda chip: [(chip, chip + 1), (chip + 1, chip)])
    near = sent(near, lambda chip: [(chip, chip + 1), (chip + 1, chip)])
    last = jnp.where(jnp.where(present(offsets, 3), core == 0, core == 1), kept, lent)
    last, cross_one, cross_zero = lax.optimization_barrier((last, cross_one, cross_zero))
    upper = sent(last, lambda chip: [(chip, far(chip) + 1)])
    lower = sent(last, lambda chip: [(chip + 1, far(chip) + 1)])
    held = list(first_round(dest_group, (own, near, cross_one, cross_zero)))
    upper, lower, cross_one, cross_zero, held[1] = lax.optimization_barrier(
        (upper, lower, cross_one, cross_zero, held[1])
    )
    passed = sent(jnp.where(present(offsets, 2), cross_one, cross_zero), lambda chip: [(chip, chip + 1)])
    return first_round(dest_group, (own, near, passed), (upper, lower), held)


def body(genotypes, dest_group):
    low_new, inverse, mix, top, low = regrouped_first_round(genotypes, dest_group)
    for cycle_round in range(1, ROUNDS):
        low_next = passed_along(low_new, "pair", 1)
        top = rotate_top(top, low, inverse, mix)
        low = low_next
        low_new, inverse, mix = rotate_low(top, low)
    low_next = passed_along(low_new, "pair", 1)
    return place_low(low_next, rotate_top(top, low, inverse, mix, 2))


def solution(mesh):
    in_specs = (P(None, ("group", "pair")), P())
    out_specs = P(None, ("group", "pair"))
    return jax.shard_map(body, mesh=mesh, in_specs=in_specs, out_specs=out_specs, check_vma=False)
```

```python
import functools

import jax
import jax.numpy as jnp
from jax import lax
from jax.experimental import pallas as pl
from jax.experimental.pallas import tpu as pltpu
from jax.sharding import PartitionSpec as P

ROUNDS = 3
SUB = 8
PANEL = 32
CHUNK = 512

epsilon = 1e-05
f32 = jnp.float32


def passed_along(array, axis, by):
    size = lax.axis_size(axis)
    return lax.ppermute(array, axis, [(i, (i + by) % size) for i in range(size)])


def dot(a, b, ca, cb):
    return lax.dot_general(
        a, b, (((ca,), (cb,)), ((), ())), precision=lax.Precision.HIGHEST, preferred_element_type=f32
    )


def dot16(a, b, ca, cb):
    return lax.dot_general(a, b, (((ca,), (cb,)), ((), ())), preferred_element_type=f32)


def identity(size):
    rows = lax.broadcasted_iota(jnp.int32, (size, size), 0)
    cols = lax.broadcasted_iota(jnp.int32, (size, size), 1)
    return (rows == cols).astype(f32)


def inverse_of(x):
    guess = pl.reciprocal(x, approx=True)
    return guess * (2.0 - x * guess)


def panel_inverse(panel, size):
    width = 4 * size
    half = 2 * size
    tile = (SUB, width)
    first = lax.broadcasted_iota(jnp.int32, tile, 1) < half
    sub = lax.broadcasted_iota(jnp.int32, tile, 0)
    count = size // SUB
    work = [panel[SUB * t : SUB * t + SUB, :] for t in range(count)]
    done = []
    for g in range(count):
        columns = []
        for j in range(SUB):
            k = SUB * g + j
            columns.append(
                {
                    t: jnp.where(
                        first,
                        jnp.broadcast_to(work[t][:, k : k + 1], tile),
                        jnp.broadcast_to(work[t][:, half + k : half + k + 1], tile),
                    )
                    for t in range(g, count)
                }
            )
        pivots = jnp.ones(tile, f32)
        for j in range(SUB):
            pivot = jnp.broadcast_to(columns[j][g][j : j + 1, :], tile)
            pivots = jnp.where(sub == j, pivot, pivots)
            inverse = inverse_of(pivot)
            row = jnp.broadcast_to(work[g][j : j + 1, :], tile)
            heads = {m: jnp.broadcast_to(columns[m][g][j : j + 1, :], tile) for m in range(j + 1, SUB)}
            for t in range(g, count):
                factor = columns[j][t] * inverse
                if t == g:
                    factor = jnp.where(sub > j, factor, 0.0)
                for m in range(j + 1, SUB):
                    columns[m][t] = columns[m][t] - factor * heads[m]
                work[t] = work[t] - factor * row
        done.append(work[g] * lax.rsqrt(pivots))
    return jnp.concatenate(done, axis=0)


def split(x):
    first = x.astype(jnp.bfloat16)
    rest = x - first.astype(f32)
    second = rest.astype(jnp.bfloat16)
    return first, second, (rest - second.astype(f32)).astype(jnp.bfloat16)


LEFT = (0, 0, 1, 0, 1, 2)
RIGHT = (0, 1, 0, 2, 1, 0)


def stacked(terms, order, axis):
    return jnp.concatenate([terms[i] for i in order], axis=axis)


def invert_factors(grams, size):
    wide = (PANEL, 4 * PANEL)
    lane = lax.broadcasted_iota(jnp.int32, wide, 1)
    sub = lax.broadcasted_iota(jnp.int32, wide, 0)
    inverse_part = lane % (2 * PANEL) >= PANEL
    eyes = (lane % (2 * PANEL) == sub + PANEL).astype(f32)
    row_lane = lax.broadcasted_iota(jnp.int32, (PANEL, size), 1)
    row_sub = lax.broadcasted_iota(jnp.int32, (PANEL, size), 0)
    all_lane = lax.broadcasted_iota(jnp.int32, (size, size), 1)
    zero = jnp.zeros((PANEL, size), f32)

    def step(index, carry):
        start = pl.multiple_of(index * PANEL, PANEL)
        stop = start + PANEL
        rows = [gram[pl.ds(start, PANEL), :] for gram in grams]
        blocks = []
        for side in range(2):
            block = rows[side][:, 0 : 4 * PANEL]
            for at in range(4 * PANEL, size, 4 * PANEL):
                block = jnp.where(start >= at, rows[side][:, at : at + 4 * PANEL], block)
            blocks.append(pltpu.roll(block, lax.rem(2 * PANEL * side + 4 * size - start, 4 * PANEL), 1))
        panel = jnp.where(inverse_part, eyes, jnp.where(lane < 2 * PANEL, blocks[0], blocks[1]))
        inverse = jnp.where(inverse_part, panel_inverse(panel, PANEL), 0.0)
        inverse = jnp.concatenate(
            [jnp.where(lane < 2 * PANEL, inverse, 0.0), jnp.where(lane >= 2 * PANEL, inverse, 0.0)], axis=0
        )
        within = (row_lane >= start) & (row_lane < stop)
        eye = (row_lane - start == row_sub).astype(f32)
        rows = [jnp.where(within, eye, part) for part in rows]
        left = split(inverse)
        right = split(jnp.concatenate([zero, rows[0], zero, rows[1]], axis=0))
        done = dot16(stacked(left, LEFT, 1), stacked(right, RIGHT, 0), 1, 0)
        terms = split(done)
        for side, gram in enumerate(grams):
            own = slice(side * PANEL, (side + 1) * PANEL)
            right = [term[own, :] for term in terms]
            left = [jnp.where(row_lane >= stop, term, jnp.zeros_like(term)) for term in right]
            change = dot16(stacked(left, LEFT, 0), stacked(right, RIGHT, 0), 0, 0)
            gram[...] = jnp.where((all_lane >= start) & (all_lane < stop), 0.0, gram[...]) - change
            gram[pl.ds(start, PANEL), :] = done[own, :]
        return carry

    lax.fori_loop(0, size // PANEL, step, 0)


def take_grams(rows, top_ref, low_ref, cross_ref, norm_ref):
    top = top_ref[rows, :]
    low = low_ref[rows, :]
    cross_ref[...] += dot16(top, low, 0, 0)
    top = top.astype(f32)
    low = low.astype(f32)
    norm_ref[0:1, :] += jnp.sum(top * top, axis=0, keepdims=True)
    norm_ref[SUB : SUB + 1, :] += jnp.sum(low * low, axis=0, keepdims=True)


def rotate(refs, outs, scratch, sems):
    top_ref, low_ref = refs
    low_out, inv_out, mix_out = outs
    cross_ref, norm_ref, gram1, gram2, new_ref, inv_ref, mix_ref = scratch
    indiv, size = top_ref.shape
    norm_top = dot(norm_ref[0:SUB, :], jnp.ones((SUB, size), f32), 0, 0)
    norm_low = norm_ref[SUB : SUB + 1, :]
    coupling = 2.0 * cross_ref[...] / (norm_top + norm_low + epsilon)
    eye = identity(size)
    gram1[...] = eye + dot(coupling, coupling, 1, 1)
    gram2[...] = eye + dot(coupling, coupling, 0, 0)
    invert_factors((gram1, gram2), size)
    below = lax.broadcasted_iota(jnp.int32, (size, size), 0) >= lax.broadcasted_iota(jnp.int32, (size, size), 1)
    inverse1 = jnp.where(below, gram1[...], 0.0)
    inverse2 = jnp.where(below, gram2[...], 0.0)
    from_top = dot(coupling, inverse2, 1, 1).astype(jnp.bfloat16)
    from_low = inverse2.astype(jnp.bfloat16)
    count = indiv // CHUNK

    def sent(step):
        rows = pl.ds(pl.multiple_of(step * CHUNK, CHUNK), CHUNK)
        return pltpu.make_async_copy(new_ref.at[rows, :], low_out.at[rows, :], sems.at[step])

    def apply(step, carry):
        rows = pl.ds(pl.multiple_of(step * CHUNK, CHUNK), CHUNK)
        new_ref[rows, :] = (
            dot16(top_ref[rows, :], from_top, 1, 0) + dot16(low_ref[rows, :], from_low, 1, 1)
        ).astype(jnp.bfloat16)
        sent(step).start()
        return carry

    lax.fori_loop(0, count, apply, 0)
    inv_ref[...] = inverse1.astype(jnp.bfloat16)
    mix_ref[...] = (-dot(inverse1, coupling, 1, 0)).astype(jnp.bfloat16)
    small = [
        pltpu.make_async_copy(inv_ref, inv_out, sems.at[count]),
        pltpu.make_async_copy(mix_ref, mix_out, sems.at[count + 1]),
    ]
    for copy in small:
        copy.start()
    for step in range(count):
        sent(step).wait()
    for copy in small:
        copy.wait()


def scratch_of(indiv, size):
    block = pltpu.VMEM((indiv, size), jnp.bfloat16)
    small = pltpu.VMEM((size, size), jnp.bfloat16)
    count = indiv // CHUNK
    return [
        block,
        block,
        pltpu.VMEM((size, size), f32),
        pltpu.VMEM((2 * SUB, size), f32),
        pltpu.VMEM((size, size), f32),
        pltpu.VMEM((size, size), f32),
        block,
        small,
        small,
        pltpu.SemaphoreType.DMA((count + 2,)),
        pltpu.SemaphoreType.DMA((2 * count,)),
    ]


def cost(indiv, size):
    return pl.CostEstimate(flops=40 * indiv * size * size, bytes_accessed=16 * indiv * size, transcendentals=0)


def round_kernel(top_hbm, low_hbm, low_out, inv_out, mix_out, top_ref, low_ref, cross_ref, norm_ref, *rest):
    *scratch, sems, in_sems = rest
    indiv, size = top_ref.shape
    count = indiv // CHUNK

    def fetched(step):
        rows = pl.ds(pl.multiple_of(step * CHUNK, CHUNK), CHUNK)
        return [
            pltpu.make_async_copy(top_hbm.at[rows, :], top_ref.at[rows, :], in_sems.at[2 * step]),
            pltpu.make_async_copy(low_hbm.at[rows, :], low_ref.at[rows, :], in_sems.at[2 * step + 1]),
        ]

    for step in range(count):
        for copy in fetched(step):
            copy.start()
    cross_ref[...] = jnp.zeros_like(cross_ref)
    norm_ref[...] = jnp.zeros_like(norm_ref)

    def accumulate(step, carry):
        for copy in fetched(step):
            copy.wait()
        take_grams(pl.ds(pl.multiple_of(step * CHUNK, CHUNK), CHUNK), top_ref, low_ref, cross_ref, norm_ref)
        return carry

    lax.fori_loop(0, count, accumulate, 0)
    rotate((top_ref, low_ref), (low_out, inv_out, mix_out), (cross_ref, norm_ref, *scratch), sems)


def rotate_low(top, low):
    indiv, size = top.shape
    square = jax.ShapeDtypeStruct((size, size), jnp.bfloat16)
    anywhere = pl.BlockSpec(memory_space=pl.ANY)
    return pl.pallas_call(
        round_kernel,
        in_specs=[anywhere] * 2,
        out_specs=[anywhere] * 3,
        out_shape=[jax.ShapeDtypeStruct((indiv, size), jnp.bfloat16), square, square],
        scratch_shapes=scratch_of(indiv, size),
        compiler_params=pltpu.CompilerParams(vmem_limit_bytes=16 * 2**20),
        cost_estimate=cost(indiv, size),
        name="rotate_low",
    )(top, low)


def offsets_of(dest):
    pair = lax.axis_index("pair")
    return dest[2 * pair], dest[2 * pair + 1]


def present(offsets, value):
    return (offsets[0] == value) | (offsets[1] == value)


def side_with(offsets, value):
    return jnp.where(offsets[1] == value, 1, 0)


def cast_kernel(dest, *refs):
    count = len(refs) // 2
    for counts_ref, out_ref in zip(refs[:count], refs[count:]):
        out_ref[...] = counts_ref[...].astype(out_ref.dtype)


def picked(genotypes, dest, wants):
    indiv, size = genotypes.shape[0], genotypes.shape[1] // 2
    steps = 4
    in_specs, out_specs, shapes = [], [], []
    for want in wants:
        parts = len(want((0, 0)))
        rows = indiv // steps // parts

        def place(i, dest, want=want):
            offsets = offsets_of(dest)
            value, *part = want(offsets)
            return (i + (part[0] * steps if part else 0), side_with(offsets, value))

        in_specs.append(pl.BlockSpec((rows, size), place))
        out_specs.append(pl.BlockSpec((rows, size), lambda i, dest: (i, 0)))
        shapes.append(jax.ShapeDtypeStruct((indiv // parts, size), jnp.bfloat16))
    return pl.pallas_call(
        cast_kernel,
        grid_spec=pltpu.PrefetchScalarGridSpec(
            num_scalar_prefetch=1, grid=(steps,), in_specs=in_specs, out_specs=out_specs
        ),
        out_shape=shapes,
        compiler_params=pltpu.CompilerParams(vmem_limit_bytes=16 * 2**20),
        name="pick_blocks",
    )(dest, *[genotypes] * len(wants))


def first_kernel(wholes, halves, dest, *refs):
    sources = refs[: wholes + halves]
    held = 5 if halves else 0
    low_out, inv_out, mix_out, top_scaled, low_scaled = refs[wholes + halves + held : wholes + halves + held + 5]
    top_ref, low_ref, cross_ref, norm_ref, *rest = refs[wholes + halves + held + 5 :]
    *scratch, sems, in_sems = rest
    indiv, size = top_ref.shape
    half = indiv // 2
    count = indiv // CHUNK

    offsets = offsets_of(dest)
    if halves:
        two = jnp.where(present(offsets, 1), wholes, 2)
        codes = (0, 1, two, jnp.where(present(offsets, 2), wholes, 2))
    else:
        codes = (0, 2, 3, 1)

    @pl.when(lax.axis_index("group") % 2 == (1 if halves else 0))
    def _():
        for side, target in enumerate((top_ref, low_ref)):
            chosen = jnp.int32(codes[0])
            for offset in range(1, 4):
                chosen = jnp.where(offsets[side] == offset, codes[offset], chosen)
            for code in range(wholes + halves // 2):
                for part in range(2):
                    rows = pl.ds(part * half, half)
                    source = sources[code].at[rows, :] if code < wholes else sources[wholes + part]

                    @pl.when(chosen == code)
                    def _():
                        pltpu.make_async_copy(source, target.at[rows, :], in_sems.at[2 * side + part]).start()

        cross_ref[...] = jnp.zeros_like(cross_ref)
        norm_ref[...] = jnp.zeros_like(norm_ref)
        scales = []
        for side, target in enumerate((top_ref, low_ref)):
            for part in range(2):
                rows = pl.ds(part * half, half)
                pltpu.make_async_copy(sources[0].at[rows, :], target.at[rows, :], in_sems.at[2 * side + part]).wait()

            def add(step, sums):
                values = target[pl.ds(pl.multiple_of(step * CHUNK, CHUNK), CHUNK), :].astype(f32)
                return (
                    sums[0] + jnp.sum(values, axis=0, keepdims=True),
                    sums[1] + jnp.sum(values * values, axis=0, keepdims=True),
                )

            total, squares = lax.fori_loop(0, count, add, (jnp.zeros((1, size), f32),) * 2)
            whole = total.astype(jnp.int32)
            spread = indiv * squares.astype(jnp.int32) - whole * whole
            variance = spread.astype(f32) * (1.0 / (indiv * indiv))
            scales.append((total * (1.0 / indiv), 1.0 / jnp.sqrt(variance + epsilon)))

        def kept(step):
            rows = pl.ds(pl.multiple_of(step * CHUNK, CHUNK), CHUNK)
            return [
                pltpu.make_async_copy(target.at[rows, :], scaled.at[rows, :], in_sems.at[4 + 2 * step + side])
                for side, (target, scaled) in enumerate(((top_ref, top_scaled), (low_ref, low_scaled)))
            ]

        def scale_rows(step, carry):
            rows = pl.ds(pl.multiple_of(step * CHUNK, CHUNK), CHUNK)
            for (mean, scale), target in zip(scales, (top_ref, low_ref)):
                target[rows, :] = ((target[rows, :].astype(f32) - mean) * scale).astype(jnp.bfloat16)
            for copy in kept(step):
                copy.start()
            take_grams(rows, top_ref, low_ref, cross_ref, norm_ref)
            return carry

        lax.fori_loop(0, count, scale_rows, 0)
        rotate((top_ref, low_ref), (low_out, inv_out, mix_out), (cross_ref, norm_ref, *scratch), sems)
        for step in range(count):
            for copy in kept(step):
                copy.wait()


def first_round(dest, wholes, halves=(), held=()):
    indiv, size = wholes[0].shape
    sources = tuple(wholes) + tuple(halves)
    block = jax.ShapeDtypeStruct((indiv, size), jnp.bfloat16)
    square = jax.ShapeDtypeStruct((size, size), jnp.bfloat16)
    anywhere = pl.BlockSpec(memory_space=pl.ANY)
    scratch = scratch_of(indiv, size)
    scratch[-1] = pltpu.SemaphoreType.DMA((2 * (indiv // CHUNK) + 4,))
    return pl.pallas_call(
        functools.partial(first_kernel, len(wholes), len(halves)),
        in_specs=[pl.BlockSpec(memory_space=pltpu.SMEM)] + [anywhere] * (len(sources) + len(held)),
        out_specs=[anywhere] * 5,
        out_shape=[block, square, square, block, block],
        input_output_aliases={1 + len(sources) + i: i for i in range(len(held))},
        scratch_shapes=scratch,
        compiler_params=pltpu.CompilerParams(vmem_limit_bytes=16 * 2**20),
        cost_estimate=cost(indiv, size),
        name="first_round",
    )(dest, *sources, *held)


def top_kernel(top_hbm, low_hbm, inv_hbm, mix_hbm, out_hbm, top_ref, low_ref, inv_ref, mix_ref, new_ref, sems):
    indiv, size = top_ref.shape
    count = indiv // CHUNK
    small = [
        pltpu.make_async_copy(inv_hbm, inv_ref, sems.at[3 * count]),
        pltpu.make_async_copy(mix_hbm, mix_ref, sems.at[3 * count + 1]),
    ]
    for copy in small:
        copy.start()

    def fetched(step):
        rows = pl.ds(pl.multiple_of(step * CHUNK, CHUNK), CHUNK)
        return [
            pltpu.make_async_copy(top_hbm.at[rows, :], top_ref.at[rows, :], sems.at[3 * step]),
            pltpu.make_async_copy(low_hbm.at[rows, :], low_ref.at[rows, :], sems.at[3 * step + 1]),
        ]

    def sent(step):
        rows = pl.ds(pl.multiple_of(step * CHUNK, CHUNK), CHUNK)
        return pltpu.make_async_copy(new_ref.at[rows, :], out_hbm.at[rows, 0:size], sems.at[3 * step + 2])

    for step in range(count):
        for copy in fetched(step):
            copy.start()
    for copy in small:
        copy.wait()

    def apply(step, carry):
        for copy in fetched(step):
            copy.wait()
        rows = pl.ds(pl.multiple_of(step * CHUNK, CHUNK), CHUNK)
        new_ref[rows, :] = (
            dot16(top_ref[rows, :], inv_ref[...], 1, 1) + dot16(low_ref[rows, :], mix_ref[...], 1, 1)
        ).astype(jnp.bfloat16)
        sent(step).start()
        return carry

    lax.fori_loop(0, count, apply, 0)
    for step in range(count):
        sent(step).wait()


def rotate_top(top, low, inverse, mix, blocks=1):
    indiv, size = top.shape
    anywhere = pl.BlockSpec(memory_space=pl.ANY)
    block = pltpu.VMEM((indiv, size), jnp.bfloat16)
    small = pltpu.VMEM((size, size), jnp.bfloat16)
    return pl.pallas_call(
        top_kernel,
        in_specs=[anywhere] * 4,
        out_specs=anywhere,
        out_shape=jax.ShapeDtypeStruct((indiv, blocks * size), jnp.bfloat16),
        scratch_shapes=[block, block, small, small, block, pltpu.SemaphoreType.DMA((3 * (indiv // CHUNK) + 2,))],
        compiler_params=pltpu.CompilerParams(vmem_limit_bytes=12 * 2**20),
        cost_estimate=pl.CostEstimate(
            flops=4 * indiv * size * size, bytes_accessed=6 * indiv * size, transcendentals=0
        ),
        name="rotate_top",
    )(top, low, inverse, mix)


def place_kernel(low_hbm, held_ref, out_hbm, low_ref, sems):
    indiv, size = low_ref.shape
    count = indiv // CHUNK
    into, out = [], []
    for step in range(count):
        rows = pl.ds(step * CHUNK, CHUNK)
        into.append(pltpu.make_async_copy(low_hbm.at[rows, :], low_ref.at[rows, :], sems.at[2 * step]))
        out.append(
            pltpu.make_async_copy(low_ref.at[rows, :], out_hbm.at[rows, size : 2 * size], sems.at[2 * step + 1])
        )
        into[-1].start()
    for step in range(count):
        into[step].wait()
        out[step].start()
    for copy in out:
        copy.wait()


def place_low(low, held):
    indiv, size = low.shape
    anywhere = pl.BlockSpec(memory_space=pl.ANY)
    return pl.pallas_call(
        place_kernel,
        in_specs=[anywhere] * 2,
        out_specs=anywhere,
        out_shape=jax.ShapeDtypeStruct(held.shape, held.dtype),
        input_output_aliases={1: 0},
        scratch_shapes=[
            pltpu.VMEM((indiv, size), jnp.bfloat16),
            pltpu.SemaphoreType.DMA((2 * (indiv // CHUNK),)),
        ],
        compiler_params=pltpu.CompilerParams(vmem_limit_bytes=4 * 2**20),
        name="place_low",
    )(low, held)


def regrouped_first_round(genotypes, dest_group):
    num_groups = lax.axis_size("group")
    core = lax.axis_index("group") % 2
    offsets = offsets_of(dest_group)

    def by_core(zero, one):
        return jnp.where(lax.axis_index("group") % 2 == 0, zero, one)

    def sent(array, hops):
        return lax.ppermute(array, "group", [hop for chip in range(0, num_groups, 2) for hop in hops(chip)])

    def far(chip):
        return (chip + 2) % num_groups

    (cross,) = picked(
        genotypes,
        dest_group,
        [lambda o: (by_core(jnp.where(present(o, 2), 2, 3), jnp.where(present(o, 1), 1, 2)),)],
    )
    cross_one = sent(cross, lambda chip: [(chip + 1, far(chip)), (chip, chip + 1)])
    cross_zero = sent(cross, lambda chip: [(chip, far(chip)), (chip + 1, chip + 1)])
    table, _ = lax.optimization_barrier((genotypes, cross))
    near, own, lent, kept = picked(
        table,
        dest_group,
        [
            lambda o: (by_core(1, 3),),
            lambda o: (0,),
            lambda o: (by_core(3, 2), by_core(1, 0)),
            lambda o: (by_core(3, 2), by_core(0, 1)),
        ],
    )
    lent = sent(lent, lambda chip: [(chip, chip + 1), (chip + 1, chip)])
    near = sent(near, lambda chip: [(chip, chip + 1), (chip + 1, chip)])
    last = jnp.where(jnp.where(present(offsets, 3), core == 0, core == 1), kept, lent)
    last, cross_one, cross_zero = lax.optimization_barrier((last, cross_one, cross_zero))
    upper = sent(last, lambda chip: [(chip, far(chip) + 1), (chip + 1, chip)])
    lower = sent(last, lambda chip: [(chip + 1, far(chip) + 1), (chip, chip)])
    passed = jnp.where(present(offsets, 2), cross_one, cross_zero)
    passed = sent(passed, lambda chip: [(chip, chip + 1), (chip + 1, chip)])
    held = list(first_round(dest_group, (own, near, cross_one, cross_zero)))
    upper, lower, held[1] = lax.optimization_barrier((upper, lower, held[1]))
    return first_round(dest_group, (own, near, passed), (upper, lower), held)


def body(genotypes, dest_group):
    low_new, inverse, mix, top, low = regrouped_first_round(genotypes, dest_group)
    for cycle_round in range(1, ROUNDS):
        low_next = passed_along(low_new, "pair", 1)
        top = rotate_top(top, low, inverse, mix)
        low = low_next
        low_new, inverse, mix = rotate_low(top, low)
    low_next = passed_along(low_new, "pair", 1)
    return place_low(low_next, rotate_top(top, low, inverse, mix, 2))


def solution(mesh):
    in_specs = (P(None, ("group", "pair")), P())
    out_specs = P(None, ("group", "pair"))
    return jax.shard_map(body, mesh=mesh, in_specs=in_specs, out_specs=out_specs, check_vma=False)
```

```python
import functools

import jax
import jax.numpy as jnp
from jax import lax
from jax.experimental import pallas as pl
from jax.experimental.pallas import tpu as pltpu
from jax.sharding import PartitionSpec as P

ROUNDS = 3
SUB = 8
PANEL = 32
LANES = 128
HALF = LANES // 2
CHUNK = 2048
PIECE = 512

epsilon = 1e-05
f32 = jnp.float32


def passed_along(array, axis, by):
    size = lax.axis_size(axis)
    return lax.ppermute(array, axis, [(i, (i + by) % size) for i in range(size)])


def dot(a, b, ca, cb):
    return lax.dot_general(
        a, b, (((ca,), (cb,)), ((), ())), precision=lax.Precision.HIGHEST, preferred_element_type=f32
    )


def dot16(a, b, ca, cb):
    return lax.dot_general(a, b, (((ca,), (cb,)), ((), ())), preferred_element_type=f32)


def identity(size):
    rows = lax.broadcasted_iota(jnp.int32, (size, size), 0)
    cols = lax.broadcasted_iota(jnp.int32, (size, size), 1)
    return (rows == cols).astype(f32)


def eliminate(block, rows):
    tile = (SUB, LANES)
    count = PANEL // SUB
    wide = rows.shape[1] // LANES
    first = lax.broadcasted_iota(jnp.int32, tile, 1) < HALF
    sub = lax.broadcasted_iota(jnp.int32, tile, 0)

    def down(value, j):
        return jnp.broadcast_to(value[j : j + 1, :], tile)

    def along(value, k):
        return jnp.where(
            first,
            jnp.broadcast_to(value[:, k : k + 1], tile),
            jnp.broadcast_to(value[:, HALF + k : HALF + k + 1], tile),
        )

    block = [block[SUB * t : SUB * t + SUB, :] for t in range(count)]
    work = [
        [rows[SUB * t : SUB * t + SUB, LANES * w : LANES * w + LANES] for w in range(wide)] for t in range(count)
    ]
    done = []
    ready = [[along(part, k) for part in block] for k in range(SUB)]
    for g in range(count):
        later = SUB * (g + 1)
        ahead = []
        if g + 1 < count:
            ahead = [[None] * (g + 1) + [along(part, later + k) for part in block[g + 1 :]] for k in range(SUB)]
        head = {(m, l): down(ready[l][g], m) for l in range(SUB) for m in range(l, SUB)}
        pivots = head[0, 0]
        for j in range(SUB):
            pivot = head[j, j]
            if j:
                pivots = jnp.where(sub == j, pivot, pivots)
            guess = pl.reciprocal(pivot, approx=True)
            mend = 2.0 - pivot * guess
            inverse = guess * mend
            for l in range(j + 1, SUB):
                for m in range(l, SUB):
                    head[m, l] = head[m, l] - (head[l, j] * head[m, j]) * guess * mend
            own = [down(part, j) for part in work[g]]
            own_block = down(block[g], j)
            for t in range(g, count):
                factor = ready[j][t] * inverse
                if t == g:
                    factor = jnp.where(sub > j, factor, 0.0)
                for m in range(j + 1, SUB):
                    ready[m][t] = ready[m][t] - factor * head[m, j]
                if t > g:
                    for k, column in enumerate(ahead):
                        column[t] = column[t] - factor * down(ready[j][g + 1], k)
                block[t] = block[t] - factor * own_block
                work[t] = [part - factor * spread for part, spread in zip(work[t], own)]
        scale = lax.rsqrt(pivots)
        done.append(jnp.concatenate([part * scale for part in work[g]], axis=1))
        ready = ahead
    return jnp.concatenate(done, axis=0)


def split(x):
    first = x.astype(jnp.bfloat16)
    rest = x - first.astype(f32)
    second = rest.astype(jnp.bfloat16)
    return first, second, (rest - second.astype(f32)).astype(jnp.bfloat16)


LEFT = (0, 0, 1, 0, 1, 2)
RIGHT = (0, 1, 0, 2, 1, 0)


def stacked(terms, order, axis):
    return jnp.concatenate([terms[i] for i in order], axis=axis)


def laced(pair):
    size = pair[0].shape[1]
    return jnp.concatenate([part[:, at : at + HALF] for at in range(0, size, HALF) for part in pair], axis=1)


def unlaced(both, side):
    size = both.shape[1]
    return jnp.concatenate([both[:, at : at + HALF] for at in range(side * HALF, size, LANES)], axis=1)


def invert_factors(gram, size):
    def columns(rows):
        lane = lax.broadcasted_iota(jnp.int32, (rows, 2 * size), 1)
        return (lane // LANES) * HALF + lane % HALF, lane % LANES < HALF

    row_column, _ = columns(PANEL)
    row_sub = lax.broadcasted_iota(jnp.int32, (PANEL, 2 * size), 0)
    part_column, part_first = columns(HALF)

    def step(index, carry):
        start = pl.multiple_of(index * PANEL, PANEL)
        stop = start + PANEL
        lanes = pl.ds(pl.multiple_of(lax.div(start, HALF) * LANES, LANES), LANES)
        block = pltpu.roll(gram[pl.ds(start, PANEL), lanes], lax.rem(LANES - lax.rem(start, HALF), LANES), 1)
        eye = (row_column - start == row_sub).astype(f32)
        within = (row_column >= start) & (row_column < stop)
        rows = eliminate(block, jnp.where(within, eye, gram[pl.ds(start, PANEL), :]))
        right = split(rows)
        left = [jnp.where(row_column >= stop, term, jnp.zeros_like(term)) for term in right]
        change = dot16(stacked(left, LEFT, 0), stacked(right, RIGHT, 0), 0, 0)
        for part in range(size // HALF):
            at = part * LANES
            own = jnp.where(part_first, change[at : at + HALF, :], change[at + HALF : at + LANES, :])
            held = pl.ds(part * HALF, HALF)
            gram[held, :] = jnp.where((part_column >= start) & (part_column < stop), 0.0, gram[held, :]) - own
        gram[pl.ds(start, PANEL), :] = rows
        return carry

    lax.fori_loop(0, size // PANEL, step, 0)


def take_grams(rows, top_ref, low_ref, cross_ref, norm_ref):
    top = top_ref[rows, :]
    low = low_ref[rows, :]
    cross_ref[...] += dot16(top, low, 0, 0)
    top = top.astype(f32)
    low = low.astype(f32)
    norm_ref[0:1, :] += jnp.sum(top * top, axis=0, keepdims=True)
    norm_ref[SUB : SUB + 1, :] += jnp.sum(low * low, axis=0, keepdims=True)


def rotate(refs, outs, scratch, sems):
    top_ref, low_ref = refs
    low_out, inv_out, mix_out = outs
    cross_ref, norm_ref, gram, new_ref, inv_ref, mix_ref = scratch
    indiv, size = top_ref.shape
    norm_top = dot(norm_ref[0:SUB, :], jnp.ones((SUB, size), f32), 0, 0)
    norm_low = norm_ref[SUB : SUB + 1, :]
    coupling = 2.0 * cross_ref[...] / (norm_top + norm_low + epsilon)
    eye = identity(size)
    gram[...] = laced((eye + dot(coupling, coupling, 1, 1), eye + dot(coupling, coupling, 0, 0)))
    invert_factors(gram, size)
    below = lax.broadcasted_iota(jnp.int32, (size, size), 0) >= lax.broadcasted_iota(jnp.int32, (size, size), 1)
    inverse1 = jnp.where(below, unlaced(gram[...], 0), 0.0)
    inverse2 = jnp.where(below, unlaced(gram[...], 1), 0.0)
    from_top = dot(coupling, inverse2, 1, 1).astype(jnp.bfloat16)
    from_low = inverse2.astype(jnp.bfloat16)
    count = indiv // CHUNK

    def sent(step):
        rows = pl.ds(pl.multiple_of(step * CHUNK, CHUNK), CHUNK)
        return pltpu.make_async_copy(new_ref.at[rows, :], low_out.at[rows, :], sems.at[step])

    def apply(step, carry):
        rows = pl.ds(pl.multiple_of(step * CHUNK, CHUNK), CHUNK)
        new_ref[rows, :] = (
            dot16(top_ref[rows, :], from_top, 1, 0) + dot16(low_ref[rows, :], from_low, 1, 1)
        ).astype(jnp.bfloat16)
        sent(step).start()
        return carry

    lax.fori_loop(0, count, apply, 0)
    inv_ref[...] = inverse1.astype(jnp.bfloat16)
    mix_ref[...] = (-dot(inverse1, coupling, 1, 0)).astype(jnp.bfloat16)
    small = [
        pltpu.make_async_copy(inv_ref, inv_out, sems.at[count]),
        pltpu.make_async_copy(mix_ref, mix_out, sems.at[count + 1]),
    ]
    for copy in small:
        copy.start()
    for step in range(count):
        sent(step).wait()
    for copy in small:
        copy.wait()


def scratch_of(indiv, size):
    block = pltpu.VMEM((indiv, size), jnp.bfloat16)
    small = pltpu.VMEM((size, size), jnp.bfloat16)
    count = indiv // CHUNK
    return [
        block,
        block,
        pltpu.VMEM((size, size), f32),
        pltpu.VMEM((2 * SUB, size), f32),
        pltpu.VMEM((size, 2 * size), f32),
        block,
        small,
        small,
        pltpu.SemaphoreType.DMA((count + 2,)),
        pltpu.SemaphoreType.DMA((2 * count,)),
    ]


def cost(indiv, size):
    return pl.CostEstimate(flops=40 * indiv * size * size, bytes_accessed=16 * indiv * size, transcendentals=0)


def start_low(lows, copy_of):
    for core, low_hbm in enumerate(lows):
        if len(lows) == 1:
            copy_of(low_hbm).start()
        else:

            @pl.when(lax.axis_index("group") % 2 == core)
            def _():
                copy_of(low_hbm).start()


def round_kernel(lows, top_hbm, *refs):
    lows, refs = refs[:lows], refs[lows:]
    low_out, inv_out, mix_out, top_ref, low_ref, cross_ref, norm_ref, *rest = refs
    *scratch, sems, in_sems = rest
    indiv, size = top_ref.shape
    count = indiv // CHUNK

    def fetch_top(step):
        rows = pl.ds(pl.multiple_of(step * CHUNK, CHUNK), CHUNK)
        return pltpu.make_async_copy(top_hbm.at[rows, :], top_ref.at[rows, :], in_sems.at[2 * step])

    def fetch_low(step, low_hbm=lows[0]):
        rows = pl.ds(pl.multiple_of(step * CHUNK, CHUNK), CHUNK)
        return pltpu.make_async_copy(low_hbm.at[rows, :], low_ref.at[rows, :], in_sems.at[2 * step + 1])

    for step in range(count):
        fetch_top(step).start()
        start_low(lows, functools.partial(fetch_low, step))
    cross_ref[...] = jnp.zeros_like(cross_ref)
    norm_ref[...] = jnp.zeros_like(norm_ref)

    def accumulate(step, carry):
        fetch_top(step).wait()
        fetch_low(step).wait()
        take_grams(pl.ds(pl.multiple_of(step * CHUNK, CHUNK), CHUNK), top_ref, low_ref, cross_ref, norm_ref)
        return carry

    lax.fori_loop(0, count, accumulate, 0)
    rotate((top_ref, low_ref), (low_out, inv_out, mix_out), (cross_ref, norm_ref, *scratch), sems)


def rotate_low(top, lows):
    indiv, size = top.shape
    square = jax.ShapeDtypeStruct((size, size), jnp.bfloat16)
    anywhere = pl.BlockSpec(memory_space=pl.ANY)
    return pl.pallas_call(
        functools.partial(round_kernel, len(lows)),
        in_specs=[anywhere] * (1 + len(lows)),
        out_specs=[anywhere] * 3,
        out_shape=[jax.ShapeDtypeStruct((indiv, size), jnp.bfloat16), square, square],
        scratch_shapes=scratch_of(indiv, size),
        compiler_params=pltpu.CompilerParams(vmem_limit_bytes=16 * 2**20),
        cost_estimate=cost(indiv, size),
        name="rotate_low",
    )(top, *lows)


def offsets_of(dest):
    pair = lax.axis_index("pair")
    return dest[2 * pair], dest[2 * pair + 1]


def present(offsets, value):
    return (offsets[0] == value) | (offsets[1] == value)


def side_with(offsets, value):
    return jnp.where(offsets[1] == value, 1, 0)


def cast_kernel(dest, *refs):
    count = len(refs) // 2
    for counts_ref, out_ref in zip(refs[:count], refs[count:]):
        out_ref[...] = counts_ref[...].astype(out_ref.dtype)


def picked(genotypes, dest, wants, room):
    indiv, size = genotypes.shape[0], genotypes.shape[1] // 2
    steps = 4
    in_specs, out_specs, shapes = [], [], []
    for want in wants:
        parts = len(want((0, 0)))
        rows = indiv // steps // parts

        def place(i, dest, want=want):
            offsets = offsets_of(dest)
            value, *part = want(offsets)
            return (i + (part[0] * steps if part else 0), side_with(offsets, value))

        in_specs.append(pl.BlockSpec((rows, size), place))
        out_specs.append(pl.BlockSpec((rows, size), lambda i, dest: (i, 0)))
        shapes.append(jax.ShapeDtypeStruct((indiv // parts, size), jnp.bfloat16))
    return pl.pallas_call(
        cast_kernel,
        grid_spec=pltpu.PrefetchScalarGridSpec(
            num_scalar_prefetch=1, grid=(steps,), in_specs=in_specs, out_specs=out_specs
        ),
        out_shape=shapes,
        compiler_params=pltpu.CompilerParams(vmem_limit_bytes=room * 2**20),
        name="pick_blocks",
    )(dest, *[genotypes] * len(wants))


def first_kernel(wholes, halves, dest, *refs):
    sources = refs[: wholes + halves]
    held = 4 if halves else 0
    low_out, inv_out, mix_out, top_scaled, low_scaled = refs[wholes + halves + held : wholes + halves + held + 5]
    top_ref, low_ref, cross_ref, norm_ref, *rest = refs[wholes + halves + held + 5 :]
    *scratch, sems, in_sems = rest
    indiv, size = top_ref.shape
    half = indiv // 2
    count = indiv // CHUNK

    offsets = offsets_of(dest)
    if halves:
        two = jnp.where(present(offsets, 1), wholes, 2)
        codes = (0, 1, two, jnp.where(present(offsets, 2), wholes, 2))
    else:
        codes = (0, 2, 3, 1)

    @pl.when(lax.axis_index("group") % 2 == (1 if halves else 0))
    def _():
        for side, target in enumerate((top_ref, low_ref)):
            chosen = jnp.int32(codes[0])
            for offset in range(1, 4):
                chosen = jnp.where(offsets[side] == offset, codes[offset], chosen)
            for code in range(wholes + halves // 2):
                for part in range(2):
                    rows = pl.ds(part * half, half)
                    source = sources[code].at[rows, :] if code < wholes else sources[wholes + part]

                    @pl.when(chosen == code)
                    def _():
                        pltpu.make_async_copy(source, target.at[rows, :], in_sems.at[2 * side + part]).start()

        cross_ref[...] = jnp.zeros_like(cross_ref)
        norm_ref[...] = jnp.zeros_like(norm_ref)
        scales = []
        for side, target in enumerate((top_ref, low_ref)):
            for part in range(2):
                rows = pl.ds(part * half, half)
                pltpu.make_async_copy(sources[0].at[rows, :], target.at[rows, :], in_sems.at[2 * side + part]).wait()

            def add(step, sums):
                values = target[pl.ds(pl.multiple_of(step * PIECE, PIECE), PIECE), :].astype(f32)
                return (
                    sums[0] + jnp.sum(values, axis=0, keepdims=True),
                    sums[1] + jnp.sum(values * values, axis=0, keepdims=True),
                )

            total, squares = lax.fori_loop(0, indiv // PIECE, add, (jnp.zeros((1, size), f32),) * 2)
            whole = total.astype(jnp.int32)
            spread = indiv * squares.astype(jnp.int32) - whole * whole
            variance = spread.astype(f32) * (1.0 / (indiv * indiv))
            scales.append((total * (1.0 / indiv), 1.0 / jnp.sqrt(variance + epsilon)))

        def kept(step):
            rows = pl.ds(pl.multiple_of(step * CHUNK, CHUNK), CHUNK)
            return [
                pltpu.make_async_copy(target.at[rows, :], scaled.at[rows, :], in_sems.at[4 + 2 * step + side])
                for side, (target, scaled) in enumerate(((top_ref, top_scaled), (low_ref, low_scaled)))
            ]

        def scale_rows(step, carry):
            rows = pl.ds(pl.multiple_of(step * CHUNK, CHUNK), CHUNK)
            for (mean, scale), target in zip(scales, (top_ref, low_ref)):
                target[rows, :] = ((target[rows, :].astype(f32) - mean) * scale).astype(jnp.bfloat16)
            for copy in kept(step):
                copy.start()
            take_grams(rows, top_ref, low_ref, cross_ref, norm_ref)
            return carry

        lax.fori_loop(0, count, scale_rows, 0)
        rotate((top_ref, low_ref), (low_out, inv_out, mix_out), (cross_ref, norm_ref, *scratch), sems)
        for step in range(count):
            for copy in kept(step):
                copy.wait()


def first_round(dest, wholes, halves=(), held=()):
    indiv, size = wholes[0].shape
    sources = tuple(wholes) + tuple(halves)
    block = jax.ShapeDtypeStruct((indiv, size), jnp.bfloat16)
    square = jax.ShapeDtypeStruct((size, size), jnp.bfloat16)
    anywhere = pl.BlockSpec(memory_space=pl.ANY)
    scratch = scratch_of(indiv, size)
    scratch[-1] = pltpu.SemaphoreType.DMA((2 * (indiv // CHUNK) + 4,))
    return pl.pallas_call(
        functools.partial(first_kernel, len(wholes), len(halves)),
        in_specs=[pl.BlockSpec(memory_space=pltpu.SMEM)] + [anywhere] * (len(sources) + len(held)),
        out_specs=[anywhere] * 5,
        out_shape=[block, square, square, block, block],
        input_output_aliases={1 + len(sources) + i: 1 + i for i in range(len(held))},
        scratch_shapes=scratch,
        compiler_params=pltpu.CompilerParams(vmem_limit_bytes=16 * 2**20),
        cost_estimate=cost(indiv, size),
        name="first_round",
    )(dest, *sources, *held)


def top_kernel(lows, top_hbm, *refs):
    lows, refs = refs[:lows], refs[lows:]
    inv_hbm, mix_hbm, out_hbm, top_ref, low_ref, inv_ref, mix_ref, new_ref, sems = refs
    indiv, size = top_ref.shape
    count = indiv // CHUNK
    small = [
        pltpu.make_async_copy(inv_hbm, inv_ref, sems.at[3 * count]),
        pltpu.make_async_copy(mix_hbm, mix_ref, sems.at[3 * count + 1]),
    ]
    for copy in small:
        copy.start()

    def fetch_top(step):
        rows = pl.ds(pl.multiple_of(step * CHUNK, CHUNK), CHUNK)
        return pltpu.make_async_copy(top_hbm.at[rows, :], top_ref.at[rows, :], sems.at[3 * step])

    def fetch_low(step, low_hbm=lows[0]):
        rows = pl.ds(pl.multiple_of(step * CHUNK, CHUNK), CHUNK)
        return pltpu.make_async_copy(low_hbm.at[rows, :], low_ref.at[rows, :], sems.at[3 * step + 1])

    def sent(step):
        rows = pl.ds(pl.multiple_of(step * CHUNK, CHUNK), CHUNK)
        return pltpu.make_async_copy(new_ref.at[rows, :], out_hbm.at[rows, 0:size], sems.at[3 * step + 2])

    for step in range(count):
        fetch_top(step).start()
        start_low(lows, functools.partial(fetch_low, step))
    for copy in small:
        copy.wait()

    def apply(step, carry):
        fetch_top(step).wait()
        fetch_low(step).wait()
        rows = pl.ds(pl.multiple_of(step * CHUNK, CHUNK), CHUNK)
        new_ref[rows, :] = (
            dot16(top_ref[rows, :], inv_ref[...], 1, 1) + dot16(low_ref[rows, :], mix_ref[...], 1, 1)
        ).astype(jnp.bfloat16)
        sent(step).start()
        return carry

    lax.fori_loop(0, count, apply, 0)
    for step in range(count):
        sent(step).wait()


def rotate_top(top, lows, inverse, mix, blocks=1):
    indiv, size = top.shape
    anywhere = pl.BlockSpec(memory_space=pl.ANY)
    block = pltpu.VMEM((indiv, size), jnp.bfloat16)
    small = pltpu.VMEM((size, size), jnp.bfloat16)
    return pl.pallas_call(
        functools.partial(top_kernel, len(lows)),
        in_specs=[anywhere] * (3 + len(lows)),
        out_specs=anywhere,
        out_shape=jax.ShapeDtypeStruct((indiv, blocks * size), jnp.bfloat16),
        scratch_shapes=[block, block, small, small, block, pltpu.SemaphoreType.DMA((3 * (indiv // CHUNK) + 2,))],
        compiler_params=pltpu.CompilerParams(vmem_limit_bytes=12 * 2**20),
        cost_estimate=pl.CostEstimate(
            flops=4 * indiv * size * size, bytes_accessed=6 * indiv * size, transcendentals=0
        ),
        name="rotate_top",
    )(top, *lows, inverse, mix)


def place_kernel(low_hbm, held_ref, out_hbm, low_ref, sems):
    indiv, size = low_ref.shape
    count = indiv // PIECE
    into, out = [], []
    for step in range(count):
        rows = pl.ds(step * PIECE, PIECE)
        into.append(pltpu.make_async_copy(low_hbm.at[rows, :], low_ref.at[rows, :], sems.at[2 * step]))
        out.append(
            pltpu.make_async_copy(low_ref.at[rows, :], out_hbm.at[rows, size : 2 * size], sems.at[2 * step + 1])
        )
        into[-1].start()
    for step in range(count):
        into[step].wait()
        out[step].start()
    for copy in out:
        copy.wait()


def place_low(low, held):
    indiv, size = low.shape
    anywhere = pl.BlockSpec(memory_space=pl.ANY)
    return pl.pallas_call(
        place_kernel,
        in_specs=[anywhere] * 2,
        out_specs=anywhere,
        out_shape=jax.ShapeDtypeStruct(held.shape, held.dtype),
        input_output_aliases={1: 0},
        scratch_shapes=[
            pltpu.VMEM((indiv, size), jnp.bfloat16),
            pltpu.SemaphoreType.DMA((2 * (indiv // PIECE),)),
        ],
        compiler_params=pltpu.CompilerParams(vmem_limit_bytes=4 * 2**20),
        name="place_low",
    )(low, held)


def next_pair(array, core):
    groups, pairs = lax.axis_size("group"), lax.axis_size("pair")
    hops = []
    for group in range(groups):
        for pair in range(pairs):
            to = (pair + 1) % pairs if group % 2 == core else pair
            hops.append((group * pairs + pair, group * pairs + to))
    return lax.ppermute(array, ("group", "pair"), hops)


def regrouped_first_round(genotypes, dest_group):
    num_groups = lax.axis_size("group")
    core = lax.axis_index("group") % 2
    offsets = offsets_of(dest_group)

    def by_core(zero, one):
        return jnp.where(lax.axis_index("group") % 2 == 0, zero, one)

    def sent(array, hops):
        return lax.ppermute(array, "group", [hop for chip in range(0, num_groups, 2) for hop in hops(chip)])

    def far(chip):
        return (chip + 2) % num_groups

    (cross,) = picked(
        genotypes,
        dest_group,
        [lambda o: (by_core(jnp.where(present(o, 2), 2, 3), jnp.where(present(o, 1), 1, 2)),)],
        56,
    )
    cross_one = sent(cross, lambda chip: [(chip + 1, far(chip)), (chip, chip + 1)])
    cross_zero = sent(cross, lambda chip: [(chip, far(chip)), (chip + 1, chip + 1)])
    table, _ = lax.optimization_barrier((genotypes, cross))
    near, own, lent, kept = picked(
        table,
        dest_group,
        [
            lambda o: (by_core(1, 3),),
            lambda o: (0,),
            lambda o: (by_core(3, 2), by_core(1, 0)),
            lambda o: (by_core(3, 2), by_core(0, 1)),
        ],
        16,
    )
    lent = sent(lent, lambda chip: [(chip, chip + 1), (chip + 1, chip)])
    near = sent(near, lambda chip: [(chip, chip + 1), (chip + 1, chip)])
    last = jnp.where(jnp.where(present(offsets, 3), core == 0, core == 1), kept, lent)
    last, cross_one, cross_zero = lax.optimization_barrier((last, cross_one, cross_zero))
    upper = sent(last, lambda chip: [(chip, far(chip) + 1), (chip + 1, chip)])
    lower = sent(last, lambda chip: [(chip + 1, far(chip) + 1), (chip, chip)])
    passed = jnp.where(present(offsets, 2), cross_one, cross_zero)
    passed = sent(passed, lambda chip: [(chip, chip + 1), (chip + 1, chip)])
    low_zero, *held = first_round(dest_group, (own, near, cross_one, cross_zero))
    low_zero, held[0] = lax.optimization_barrier((low_zero, held[0]))
    low_zero = next_pair(low_zero, 0)
    upper, lower, held[0] = lax.optimization_barrier((upper, lower, held[0]))
    low_one, *held = first_round(dest_group, (own, near, passed), (upper, lower), held)
    return (low_zero, next_pair(low_one, 1)), *held


def body(genotypes, dest_group):
    low_next, inverse, mix, top, low = regrouped_first_round(genotypes, dest_group)
    top = rotate_top(top, (low,), inverse, mix)
    for cycle_round in range(1, ROUNDS):
        low_new, inverse, mix = rotate_low(top, low_next)
        low, low_next = low_next, (passed_along(low_new, "pair", 1),)
        if cycle_round < ROUNDS - 1:
            top = rotate_top(top, low, inverse, mix)
    return place_low(low_next[0], rotate_top(top, low, inverse, mix, 2))


def solution(mesh):
    in_specs = (P(None, ("group", "pair")), P())
    out_specs = P(None, ("group", "pair"))
    return jax.shard_map(body, mesh=mesh, in_specs=in_specs, out_specs=out_specs, check_vma=False)
```

```python
import functools

import jax
import jax.numpy as jnp
from jax import lax
from jax.experimental import pallas as pl
from jax.experimental.pallas import tpu as pltpu
from jax.sharding import PartitionSpec as P

ROUNDS = 3
SUB = 8
PANEL = 32
LANES = 128
HALF = LANES // 2
CHUNK = 2048
PIECE = 512

epsilon = 1e-05
f32 = jnp.float32


def passed_along(array, axis, by):
    size = lax.axis_size(axis)
    return lax.ppermute(array, axis, [(i, (i + by) % size) for i in range(size)])


def dot(a, b, ca, cb):
    return lax.dot_general(
        a, b, (((ca,), (cb,)), ((), ())), precision=lax.Precision.HIGHEST, preferred_element_type=f32
    )


def dot16(a, b, ca, cb):
    return lax.dot_general(a, b, (((ca,), (cb,)), ((), ())), preferred_element_type=f32)


def identity(size):
    rows = lax.broadcasted_iota(jnp.int32, (size, size), 0)
    cols = lax.broadcasted_iota(jnp.int32, (size, size), 1)
    return (rows == cols).astype(f32)


def eliminate(block, rows):
    tile = (SUB, LANES)
    count = PANEL // SUB
    wide = rows.shape[1] // LANES
    first = lax.broadcasted_iota(jnp.int32, tile, 1) < HALF
    sub = lax.broadcasted_iota(jnp.int32, tile, 0)

    def down(value, j):
        return jnp.broadcast_to(value[j : j + 1, :], tile)

    def along(value, k):
        return jnp.where(
            first,
            jnp.broadcast_to(value[:, k : k + 1], tile),
            jnp.broadcast_to(value[:, HALF + k : HALF + k + 1], tile),
        )

    block = [block[SUB * t : SUB * t + SUB, :] for t in range(count)]
    work = [
        [rows[SUB * t : SUB * t + SUB, LANES * w : LANES * w + LANES] for w in range(wide)] for t in range(count)
    ]
    done = []
    ready = [[along(part, k) for part in block] for k in range(SUB)]
    for g in range(count):
        later = SUB * (g + 1)
        ahead = []
        if g + 1 < count:
            ahead = [[None] * (g + 1) + [along(part, later + k) for part in block[g + 1 :]] for k in range(SUB)]
        head = {(m, l): down(ready[l][g], m) for l in range(SUB) for m in range(l, SUB)}
        pivots = head[0, 0]
        for j in range(SUB):
            pivot = head[j, j]
            if j:
                pivots = jnp.where(sub == j, pivot, pivots)
            guess = pl.reciprocal(pivot, approx=True)
            mend = 2.0 - pivot * guess
            inverse = guess * mend
            for l in range(j + 1, SUB):
                for m in range(l, SUB):
                    head[m, l] = head[m, l] - (head[l, j] * head[m, j]) * guess * mend
            own = [down(part, j) for part in work[g]]
            own_block = down(block[g], j)
            for t in range(g, count):
                factor = ready[j][t] * inverse
                if t == g:
                    factor = jnp.where(sub > j, factor, 0.0)
                for m in range(j + 1, SUB):
                    ready[m][t] = ready[m][t] - factor * head[m, j]
                if t > g:
                    for k, column in enumerate(ahead):
                        column[t] = column[t] - factor * down(ready[j][g + 1], k)
                block[t] = block[t] - factor * own_block
                work[t] = [part - factor * spread for part, spread in zip(work[t], own)]
        scale = lax.rsqrt(pivots)
        done.append(jnp.concatenate([part * scale for part in work[g]], axis=1))
        ready = ahead
    return jnp.concatenate(done, axis=0)


def split(x):
    first = x.astype(jnp.bfloat16)
    rest = x - first.astype(f32)
    second = rest.astype(jnp.bfloat16)
    return first, second, (rest - second.astype(f32)).astype(jnp.bfloat16)


LEFT = (0, 0, 1, 0, 1, 2)
RIGHT = (0, 1, 0, 2, 1, 0)


def stacked(terms, order, axis):
    return jnp.concatenate([terms[i] for i in order], axis=axis)


def laced(pair):
    size = pair[0].shape[1]
    return jnp.concatenate([part[:, at : at + HALF] for at in range(0, size, HALF) for part in pair], axis=1)


def unlaced(both, side):
    size = both.shape[1]
    return jnp.concatenate([both[:, at : at + HALF] for at in range(side * HALF, size, LANES)], axis=1)


def invert_factors(gram, size):
    def columns(rows):
        lane = lax.broadcasted_iota(jnp.int32, (rows, 2 * size), 1)
        return (lane // LANES) * HALF + lane % HALF, lane % LANES < HALF

    row_column, _ = columns(PANEL)
    row_sub = lax.broadcasted_iota(jnp.int32, (PANEL, 2 * size), 0)
    part_column, part_first = columns(HALF)
    part_sub = lax.broadcasted_iota(jnp.int32, (HALF, 2 * size), 0)

    def step(index, carry):
        start = pl.multiple_of(index * PANEL, PANEL)
        stop = start + PANEL
        lanes = pl.ds(pl.multiple_of(lax.div(start, HALF) * LANES, LANES), LANES)
        block = pltpu.roll(gram[pl.ds(start, PANEL), lanes], lax.rem(LANES - lax.rem(start, HALF), LANES), 1)
        eye = (row_column - start == row_sub).astype(f32)
        within = (row_column >= start) & (row_column < stop)
        rows = eliminate(block, jnp.where(within, eye, gram[pl.ds(start, PANEL), :]))
        gram[pl.ds(start, PANEL), :] = rows

        @pl.when(stop < size)
        def _():
            right = split(rows)
            left = [jnp.where(row_column >= stop, term, jnp.zeros_like(term)) for term in right]
            change = dot16(stacked(left, LEFT, 0), stacked(right, RIGHT, 0), 0, 0)
            done = (part_column >= start) & (part_column < stop)
            for part in range(size // HALF):
                at = part * LANES
                own = jnp.where(part_first, change[at : at + HALF, :], change[at + HALF : at + LANES, :])
                held = pl.ds(part * HALF, HALF)
                gram[held, :] = jnp.where(done & (part * HALF + part_sub >= stop), 0.0, gram[held, :]) - own

        return carry

    lax.fori_loop(0, size // PANEL, step, 0)


def take_grams(rows, top_ref, low_ref, cross_ref, norm_ref):
    top = top_ref[rows, :]
    low = low_ref[rows, :]
    cross_ref[...] += dot16(top, low, 0, 0)
    top = top.astype(f32)
    low = low.astype(f32)
    norm_ref[0:1, :] += jnp.sum(top * top, axis=0, keepdims=True)
    norm_ref[SUB : SUB + 1, :] += jnp.sum(low * low, axis=0, keepdims=True)


def rotate(refs, outs, scratch, sems):
    top_ref, low_ref = refs
    low_out, inv_out, mix_out = outs
    cross_ref, norm_ref, gram, new_ref, inv_ref, mix_ref = scratch
    indiv, size = top_ref.shape
    norm_top = dot(norm_ref[0:SUB, :], jnp.ones((SUB, size), f32), 0, 0)
    norm_low = norm_ref[SUB : SUB + 1, :]
    coupling = 2.0 * cross_ref[...] / (norm_top + norm_low + epsilon)
    eye = identity(size)
    gram[...] = laced((eye + dot(coupling, coupling, 1, 1), eye + dot(coupling, coupling, 0, 0)))
    invert_factors(gram, size)
    below = lax.broadcasted_iota(jnp.int32, (size, size), 0) >= lax.broadcasted_iota(jnp.int32, (size, size), 1)
    inverse1 = jnp.where(below, unlaced(gram[...], 0), 0.0)
    inverse2 = jnp.where(below, unlaced(gram[...], 1), 0.0)
    from_top = dot(coupling, inverse2, 1, 1).astype(jnp.bfloat16)
    from_low = inverse2.astype(jnp.bfloat16)
    count = indiv // CHUNK

    def sent(step):
        rows = pl.ds(pl.multiple_of(step * CHUNK, CHUNK), CHUNK)
        return pltpu.make_async_copy(new_ref.at[rows, :], low_out.at[rows, :], sems.at[step])

    def apply(step, carry):
        rows = pl.ds(pl.multiple_of(step * CHUNK, CHUNK), CHUNK)
        new_ref[rows, :] = (
            dot16(top_ref[rows, :], from_top, 1, 0) + dot16(low_ref[rows, :], from_low, 1, 1)
        ).astype(jnp.bfloat16)
        sent(step).start()
        return carry

    lax.fori_loop(0, count, apply, 0)
    inv_ref[...] = inverse1.astype(jnp.bfloat16)
    mix_ref[...] = (-dot(inverse1, coupling, 1, 0)).astype(jnp.bfloat16)
    small = [
        pltpu.make_async_copy(inv_ref, inv_out, sems.at[count]),
        pltpu.make_async_copy(mix_ref, mix_out, sems.at[count + 1]),
    ]
    for copy in small:
        copy.start()
    for step in range(count):
        sent(step).wait()
    for copy in small:
        copy.wait()


def scratch_of(indiv, size):
    block = pltpu.VMEM((indiv, size), jnp.bfloat16)
    small = pltpu.VMEM((size, size), jnp.bfloat16)
    count = indiv // CHUNK
    return [
        block,
        block,
        pltpu.VMEM((size, size), f32),
        pltpu.VMEM((2 * SUB, size), f32),
        pltpu.VMEM((size, 2 * size), f32),
        block,
        small,
        small,
        pltpu.SemaphoreType.DMA((count + 2,)),
        pltpu.SemaphoreType.DMA((2 * count,)),
    ]


def cost(indiv, size):
    return pl.CostEstimate(flops=40 * indiv * size * size, bytes_accessed=16 * indiv * size, transcendentals=0)


def start_low(lows, copy_of):
    for core, low_hbm in enumerate(lows):
        if len(lows) == 1:
            copy_of(low_hbm).start()
        else:

            @pl.when(lax.axis_index("group") % 2 == core)
            def _():
                copy_of(low_hbm).start()


def round_kernel(lows, top_hbm, *refs):
    lows, refs = refs[:lows], refs[lows:]
    low_out, inv_out, mix_out, top_ref, low_ref, cross_ref, norm_ref, *rest = refs
    *scratch, sems, in_sems = rest
    indiv, size = top_ref.shape
    count = indiv // CHUNK

    def fetch_top(step):
        rows = pl.ds(pl.multiple_of(step * CHUNK, CHUNK), CHUNK)
        return pltpu.make_async_copy(top_hbm.at[rows, :], top_ref.at[rows, :], in_sems.at[2 * step])

    def fetch_low(step, low_hbm=lows[0]):
        rows = pl.ds(pl.multiple_of(step * CHUNK, CHUNK), CHUNK)
        return pltpu.make_async_copy(low_hbm.at[rows, :], low_ref.at[rows, :], in_sems.at[2 * step + 1])

    for step in range(count):
        fetch_top(step).start()
        start_low(lows, functools.partial(fetch_low, step))
    cross_ref[...] = jnp.zeros_like(cross_ref)
    norm_ref[...] = jnp.zeros_like(norm_ref)

    def accumulate(step, carry):
        fetch_top(step).wait()
        fetch_low(step).wait()
        take_grams(pl.ds(pl.multiple_of(step * CHUNK, CHUNK), CHUNK), top_ref, low_ref, cross_ref, norm_ref)
        return carry

    lax.fori_loop(0, count, accumulate, 0)
    rotate((top_ref, low_ref), (low_out, inv_out, mix_out), (cross_ref, norm_ref, *scratch), sems)


def rotate_low(top, lows):
    indiv, size = top.shape
    square = jax.ShapeDtypeStruct((size, size), jnp.bfloat16)
    anywhere = pl.BlockSpec(memory_space=pl.ANY)
    return pl.pallas_call(
        functools.partial(round_kernel, len(lows)),
        in_specs=[anywhere] * (1 + len(lows)),
        out_specs=[anywhere] * 3,
        out_shape=[jax.ShapeDtypeStruct((indiv, size), jnp.bfloat16), square, square],
        scratch_shapes=scratch_of(indiv, size),
        compiler_params=pltpu.CompilerParams(vmem_limit_bytes=16 * 2**20),
        cost_estimate=cost(indiv, size),
        name="rotate_low",
    )(top, *lows)


def offsets_of(dest):
    pair = lax.axis_index("pair")
    return dest[2 * pair], dest[2 * pair + 1]


def present(offsets, value):
    return (offsets[0] == value) | (offsets[1] == value)


def side_with(offsets, value):
    return jnp.where(offsets[1] == value, 1, 0)


def cross_kernel(dest, counts_hbm, out_hbm, counts_ref, cast_ref, sems):
    indiv, size = cast_ref.shape
    steps = indiv // PIECE
    offsets = offsets_of(dest)
    core = lax.axis_index("group") % 2
    zero = jnp.where(present(offsets, 2), 2, 3)
    one = jnp.where(present(offsets, 1), 1, 2)
    column = pl.multiple_of(side_with(offsets, jnp.where(core == 0, zero, one)) * size, size)

    def fetched(step):
        rows = pl.ds(step * PIECE, PIECE)
        return pltpu.make_async_copy(
            counts_hbm.at[rows, pl.ds(column, size)], counts_ref.at[rows, :], sems.at[2 * step]
        )

    def sent(step):
        rows = pl.ds(step * PIECE, PIECE)
        return pltpu.make_async_copy(cast_ref.at[rows, :], out_hbm.at[rows, :], sems.at[2 * step + 1])

    for step in range(steps):
        fetched(step).start()
    for step in range(steps):
        rows = pl.ds(step * PIECE, PIECE)
        fetched(step).wait()
        cast_ref[rows, :] = counts_ref[rows, :].astype(cast_ref.dtype)
        sent(step).start()
    for step in range(steps):
        sent(step).wait()


def picked_cross(genotypes, dest):
    indiv, size = genotypes.shape[0], genotypes.shape[1] // 2
    return pl.pallas_call(
        cross_kernel,
        in_specs=[pl.BlockSpec(memory_space=pltpu.SMEM), pl.BlockSpec(memory_space=pl.ANY)],
        out_specs=pl.BlockSpec(memory_space=pl.ANY),
        out_shape=jax.ShapeDtypeStruct((indiv, size), jnp.bfloat16),
        scratch_shapes=[
            pltpu.VMEM((indiv, size), jnp.int32),
            pltpu.VMEM((indiv, size), jnp.bfloat16),
            pltpu.SemaphoreType.DMA((2 * (indiv // PIECE),)),
        ],
        compiler_params=pltpu.CompilerParams(vmem_limit_bytes=56 * 2**20),
        name="pick_cross",
    )(dest, genotypes)


def cast_kernel(dest, *refs):
    count = len(refs) // 2
    for counts_ref, out_ref in zip(refs[:count], refs[count:]):
        out_ref[...] = counts_ref[...].astype(out_ref.dtype)


def picked(genotypes, dest, wants):
    indiv, size = genotypes.shape[0], genotypes.shape[1] // 2
    steps = 4
    in_specs, out_specs, shapes = [], [], []
    for want in wants:
        parts = len(want((0, 0)))
        rows = indiv // steps // parts

        def place(i, dest, want=want):
            offsets = offsets_of(dest)
            value, *part = want(offsets)
            return (i + (part[0] * steps if part else 0), side_with(offsets, value))

        in_specs.append(pl.BlockSpec((rows, size), place))
        out_specs.append(pl.BlockSpec((rows, size), lambda i, dest: (i, 0)))
        shapes.append(jax.ShapeDtypeStruct((indiv // parts, size), jnp.bfloat16))
    return pl.pallas_call(
        cast_kernel,
        grid_spec=pltpu.PrefetchScalarGridSpec(
            num_scalar_prefetch=1, grid=(steps,), in_specs=in_specs, out_specs=out_specs
        ),
        out_shape=shapes,
        compiler_params=pltpu.CompilerParams(vmem_limit_bytes=16 * 2**20),
        name="pick_blocks",
    )(dest, *[genotypes] * len(wants))


def first_kernel(wholes, halves, dest, *refs):
    sources = refs[: wholes + halves]
    held = 4 if halves else 0
    low_out, inv_out, mix_out, top_scaled, low_scaled = refs[wholes + halves + held : wholes + halves + held + 5]
    top_ref, low_ref, cross_ref, norm_ref, *rest = refs[wholes + halves + held + 5 :]
    *scratch, sems, in_sems = rest
    indiv, size = top_ref.shape
    half = indiv // 2
    count = indiv // CHUNK

    offsets = offsets_of(dest)
    if halves:
        two = jnp.where(present(offsets, 1), wholes, 2)
        codes = (0, 1, two, jnp.where(present(offsets, 2), wholes, 2))
    else:
        codes = (0, 2, 3, 1)

    @pl.when(lax.axis_index("group") % 2 == (1 if halves else 0))
    def _():
        for side, target in enumerate((top_ref, low_ref)):
            chosen = jnp.int32(codes[0])
            for offset in range(1, 4):
                chosen = jnp.where(offsets[side] == offset, codes[offset], chosen)
            for code in range(wholes + halves // 2):
                for part in range(2):
                    rows = pl.ds(part * half, half)
                    source = sources[code].at[rows, :] if code < wholes else sources[wholes + part]

                    @pl.when(chosen == code)
                    def _():
                        pltpu.make_async_copy(source, target.at[rows, :], in_sems.at[2 * side + part]).start()

        cross_ref[...] = jnp.zeros_like(cross_ref)
        norm_ref[...] = jnp.zeros_like(norm_ref)
        for side, target in enumerate((top_ref, low_ref)):
            for part in range(2):
                rows = pl.ds(part * half, half)
                pltpu.make_async_copy(sources[0].at[rows, :], target.at[rows, :], in_sems.at[2 * side + part]).wait()

        def add(step, sums):
            rows = pl.ds(pl.multiple_of(step * PIECE, PIECE), PIECE)
            new = []
            for side, target in enumerate((top_ref, low_ref)):
                values = target[rows, :].astype(f32).reshape(PIECE // SUB, SUB, size)
                new += [sums[2 * side] + jnp.sum(values, axis=0)]
                new += [sums[2 * side + 1] + jnp.sum(values * values, axis=0)]
            return tuple(new)

        sums = lax.fori_loop(0, indiv // PIECE, add, (jnp.zeros((SUB, size), f32),) * 4)
        sums = [jnp.sum(part, axis=0, keepdims=True) for part in sums]
        scales = []
        for total, squares in (sums[0:2], sums[2:4]):
            whole = total.astype(jnp.int32)
            spread = indiv * squares.astype(jnp.int32) - whole * whole
            variance = spread.astype(f32) * (1.0 / (indiv * indiv))
            scales.append((total * (1.0 / indiv), 1.0 / jnp.sqrt(variance + epsilon)))

        def kept(step):
            rows = pl.ds(pl.multiple_of(step * CHUNK, CHUNK), CHUNK)
            return [
                pltpu.make_async_copy(target.at[rows, :], scaled.at[rows, :], in_sems.at[4 + 2 * step + side])
                for side, (target, scaled) in enumerate(((top_ref, top_scaled), (low_ref, low_scaled)))
            ]

        def scale_rows(step, carry):
            rows = pl.ds(pl.multiple_of(step * CHUNK, CHUNK), CHUNK)
            for (mean, scale), target in zip(scales, (top_ref, low_ref)):
                target[rows, :] = ((target[rows, :].astype(f32) - mean) * scale).astype(jnp.bfloat16)
            for copy in kept(step):
                copy.start()
            take_grams(rows, top_ref, low_ref, cross_ref, norm_ref)
            return carry

        lax.fori_loop(0, count, scale_rows, 0)
        rotate((top_ref, low_ref), (low_out, inv_out, mix_out), (cross_ref, norm_ref, *scratch), sems)
        for step in range(count):
            for copy in kept(step):
                copy.wait()


def first_round(dest, wholes, halves=(), held=()):
    indiv, size = wholes[0].shape
    sources = tuple(wholes) + tuple(halves)
    block = jax.ShapeDtypeStruct((indiv, size), jnp.bfloat16)
    square = jax.ShapeDtypeStruct((size, size), jnp.bfloat16)
    anywhere = pl.BlockSpec(memory_space=pl.ANY)
    scratch = scratch_of(indiv, size)
    scratch[-1] = pltpu.SemaphoreType.DMA((2 * (indiv // CHUNK) + 4,))
    return pl.pallas_call(
        functools.partial(first_kernel, len(wholes), len(halves)),
        in_specs=[pl.BlockSpec(memory_space=pltpu.SMEM)] + [anywhere] * (len(sources) + len(held)),
        out_specs=[anywhere] * 5,
        out_shape=[block, square, square, block, block],
        input_output_aliases={1 + len(sources) + i: 1 + i for i in range(len(held))},
        scratch_shapes=scratch,
        compiler_params=pltpu.CompilerParams(vmem_limit_bytes=16 * 2**20),
        cost_estimate=cost(indiv, size),
        name="first_round",
    )(dest, *sources, *held)


def top_kernel(lows, top_hbm, *refs):
    lows, refs = refs[:lows], refs[lows:]
    inv_hbm, mix_hbm, out_hbm, top_ref, low_ref, inv_ref, mix_ref, new_ref, sems = refs
    indiv, size = top_ref.shape
    count = indiv // CHUNK
    small = [
        pltpu.make_async_copy(inv_hbm, inv_ref, sems.at[3 * count]),
        pltpu.make_async_copy(mix_hbm, mix_ref, sems.at[3 * count + 1]),
    ]
    for copy in small:
        copy.start()

    def fetch_top(step):
        rows = pl.ds(pl.multiple_of(step * CHUNK, CHUNK), CHUNK)
        return pltpu.make_async_copy(top_hbm.at[rows, :], top_ref.at[rows, :], sems.at[3 * step])

    def fetch_low(step, low_hbm=lows[0]):
        rows = pl.ds(pl.multiple_of(step * CHUNK, CHUNK), CHUNK)
        return pltpu.make_async_copy(low_hbm.at[rows, :], low_ref.at[rows, :], sems.at[3 * step + 1])

    def sent(step):
        rows = pl.ds(pl.multiple_of(step * CHUNK, CHUNK), CHUNK)
        return pltpu.make_async_copy(new_ref.at[rows, :], out_hbm.at[rows, 0:size], sems.at[3 * step + 2])

    for step in range(count):
        fetch_top(step).start()
        start_low(lows, functools.partial(fetch_low, step))
    for copy in small:
        copy.wait()

    def apply(step, carry):
        fetch_top(step).wait()
        fetch_low(step).wait()
        rows = pl.ds(pl.multiple_of(step * CHUNK, CHUNK), CHUNK)
        new_ref[rows, :] = (
            dot16(top_ref[rows, :], inv_ref[...], 1, 1) + dot16(low_ref[rows, :], mix_ref[...], 1, 1)
        ).astype(jnp.bfloat16)
        sent(step).start()
        return carry

    lax.fori_loop(0, count, apply, 0)
    for step in range(count):
        sent(step).wait()


def rotate_top(top, lows, inverse, mix, blocks=1):
    indiv, size = top.shape
    anywhere = pl.BlockSpec(memory_space=pl.ANY)
    block = pltpu.VMEM((indiv, size), jnp.bfloat16)
    small = pltpu.VMEM((size, size), jnp.bfloat16)
    return pl.pallas_call(
        functools.partial(top_kernel, len(lows)),
        in_specs=[anywhere] * (3 + len(lows)),
        out_specs=anywhere,
        out_shape=jax.ShapeDtypeStruct((indiv, blocks * size), jnp.bfloat16),
        scratch_shapes=[block, block, small, small, block, pltpu.SemaphoreType.DMA((3 * (indiv // CHUNK) + 2,))],
        compiler_params=pltpu.CompilerParams(vmem_limit_bytes=12 * 2**20),
        cost_estimate=pl.CostEstimate(
            flops=4 * indiv * size * size, bytes_accessed=6 * indiv * size, transcendentals=0
        ),
        name="rotate_top",
    )(top, *lows, inverse, mix)


def place_kernel(low_hbm, held_ref, out_hbm, low_ref, sems):
    indiv, size = low_ref.shape
    count = indiv // PIECE
    into, out = [], []
    for step in range(count):
        rows = pl.ds(step * PIECE, PIECE)
        into.append(pltpu.make_async_copy(low_hbm.at[rows, :], low_ref.at[rows, :], sems.at[2 * step]))
        out.append(
            pltpu.make_async_copy(low_ref.at[rows, :], out_hbm.at[rows, size : 2 * size], sems.at[2 * step + 1])
        )
        into[-1].start()
    for step in range(count):
        into[step].wait()
        out[step].start()
    for copy in out:
        copy.wait()


def place_low(low, held):
    indiv, size = low.shape
    anywhere = pl.BlockSpec(memory_space=pl.ANY)
    return pl.pallas_call(
        place_kernel,
        in_specs=[anywhere] * 2,
        out_specs=anywhere,
        out_shape=jax.ShapeDtypeStruct(held.shape, held.dtype),
        input_output_aliases={1: 0},
        scratch_shapes=[
            pltpu.VMEM((indiv, size), jnp.bfloat16),
            pltpu.SemaphoreType.DMA((2 * (indiv // PIECE),)),
        ],
        compiler_params=pltpu.CompilerParams(vmem_limit_bytes=4 * 2**20),
        name="place_low",
    )(low, held)


def next_pair(array, core):
    groups, pairs = lax.axis_size("group"), lax.axis_size("pair")
    hops = []
    for group in range(groups):
        for pair in range(pairs):
            to = (pair + 1) % pairs if group % 2 == core else pair
            hops.append((group * pairs + pair, group * pairs + to))
    return lax.ppermute(array, ("group", "pair"), hops)


def regrouped_first_round(genotypes, dest_group):
    num_groups = lax.axis_size("group")
    core = lax.axis_index("group") % 2
    offsets = offsets_of(dest_group)

    def by_core(zero, one):
        return jnp.where(lax.axis_index("group") % 2 == 0, zero, one)

    def sent(array, hops):
        return lax.ppermute(array, "group", [hop for chip in range(0, num_groups, 2) for hop in hops(chip)])

    def far(chip):
        return (chip + 2) % num_groups

    cross = picked_cross(genotypes, dest_group)
    cross_one = sent(cross, lambda chip: [(chip + 1, far(chip)), (chip, chip + 1)])
    cross_zero = sent(cross, lambda chip: [(chip, far(chip)), (chip + 1, chip + 1)])
    table, _ = lax.optimization_barrier((genotypes, cross))
    near, own, lent, kept = picked(
        table,
        dest_group,
        [
            lambda o: (by_core(1, 3),),
            lambda o: (0,),
            lambda o: (by_core(3, 2), by_core(1, 0)),
            lambda o: (by_core(3, 2), by_core(0, 1)),
        ],
    )
    lent = sent(lent, lambda chip: [(chip, chip + 1), (chip + 1, chip)])
    near = sent(near, lambda chip: [(chip, chip + 1), (chip + 1, chip)])
    last = jnp.where(jnp.where(present(offsets, 3), core == 0, core == 1), kept, lent)
    last, cross_one, cross_zero = lax.optimization_barrier((last, cross_one, cross_zero))
    upper = sent(last, lambda chip: [(chip, far(chip) + 1), (chip + 1, chip)])
    lower = sent(last, lambda chip: [(chip + 1, far(chip) + 1), (chip, chip)])
    passed = jnp.where(present(offsets, 2), cross_one, cross_zero)
    passed = sent(passed, lambda chip: [(chip, chip + 1), (chip + 1, chip)])
    low_zero, *held = first_round(dest_group, (own, near, cross_one, cross_zero))
    low_zero, held[0] = lax.optimization_barrier((low_zero, held[0]))
    low_zero = next_pair(low_zero, 0)
    upper, lower, held[0] = lax.optimization_barrier((upper, lower, held[0]))
    low_one, *held = first_round(dest_group, (own, near, passed), (upper, lower), held)
    return (low_zero, next_pair(low_one, 1)), *held


def body(genotypes, dest_group):
    low_next, inverse, mix, top, low = regrouped_first_round(genotypes, dest_group)
    top = rotate_top(top, (low,), inverse, mix)
    for cycle_round in range(1, ROUNDS):
        low_new, inverse, mix = rotate_low(top, low_next)
        low, low_next = low_next, (passed_along(low_new, "pair", 1),)
        if cycle_round < ROUNDS - 1:
            top = rotate_top(top, low, inverse, mix)
    return place_low(low_next[0], rotate_top(top, low, inverse, mix, 2))


def solution(mesh):
    in_specs = (P(None, ("group", "pair")), P())
    out_specs = P(None, ("group", "pair"))
    return jax.shard_map(body, mesh=mesh, in_specs=in_specs, out_specs=out_specs, check_vma=False)
```

```python
import functools

import jax
import jax.numpy as jnp
from jax import lax
from jax.experimental import pallas as pl
from jax.experimental.pallas import tpu as pltpu
from jax.sharding import PartitionSpec as P

ROUNDS = 3
SUB = 8
PANEL = 32
LANES = 128
HALF = LANES // 2
CHUNK = 2048
PIECE = 512
TALL = 16
GROUP = 32

epsilon = 1e-05
f32 = jnp.float32


def passed_along(array, axis, by):
    size = lax.axis_size(axis)
    return lax.ppermute(array, axis, [(i, (i + by) % size) for i in range(size)])


def dot(a, b, ca, cb):
    return lax.dot_general(
        a, b, (((ca,), (cb,)), ((), ())), precision=lax.Precision.HIGHEST, preferred_element_type=f32
    )


def dot16(a, b, ca, cb):
    return lax.dot_general(a, b, (((ca,), (cb,)), ((), ())), preferred_element_type=f32)


def identity(size):
    rows = lax.broadcasted_iota(jnp.int32, (size, size), 0)
    cols = lax.broadcasted_iota(jnp.int32, (size, size), 1)
    return (rows == cols).astype(f32)


def eliminate(block, rows):
    tile = (SUB, LANES)
    count = PANEL // SUB
    wide = rows.shape[1] // LANES
    first = lax.broadcasted_iota(jnp.int32, tile, 1) < HALF
    sub = lax.broadcasted_iota(jnp.int32, tile, 0)

    def down(value, j):
        return jnp.broadcast_to(value[j : j + 1, :], tile)

    def along(value, k):
        return jnp.where(
            first,
            jnp.broadcast_to(value[:, k : k + 1], tile),
            jnp.broadcast_to(value[:, HALF + k : HALF + k + 1], tile),
        )

    block = [block[SUB * t : SUB * t + SUB, :] for t in range(count)]
    work = [
        [rows[SUB * t : SUB * t + SUB, LANES * w : LANES * w + LANES] for w in range(wide)] for t in range(count)
    ]
    done = []
    ready = [[along(part, k) for part in block] for k in range(SUB)]
    for g in range(count):
        later = SUB * (g + 1)
        ahead = []
        if g + 1 < count:
            ahead = [[None] * (g + 1) + [along(part, later + k) for part in block[g + 1 :]] for k in range(SUB)]
        head = {(m, l): down(ready[l][g], m) for l in range(SUB) for m in range(l, SUB)}
        pivots = head[0, 0]
        for j in range(SUB):
            pivot = head[j, j]
            if j:
                pivots = jnp.where(sub == j, pivot, pivots)
            guess = pl.reciprocal(pivot, approx=True)
            mend = 2.0 - pivot * guess
            inverse = guess * mend
            for l in range(j + 1, SUB):
                for m in range(l, SUB):
                    head[m, l] = head[m, l] - (head[l, j] * head[m, j]) * guess * mend
            own = [down(part, j) for part in work[g]]
            own_block = down(block[g], j)
            for t in range(g, count):
                factor = ready[j][t] * inverse
                if t == g:
                    factor = jnp.where(sub > j, factor, 0.0)
                for m in range(j + 1, SUB):
                    ready[m][t] = ready[m][t] - factor * head[m, j]
                if t > g:
                    for k, column in enumerate(ahead):
                        column[t] = column[t] - factor * down(ready[j][g + 1], k)
                block[t] = block[t] - factor * own_block
                work[t] = [part - factor * spread for part, spread in zip(work[t], own)]
        scale = lax.rsqrt(pivots)
        done.append(jnp.concatenate([part * scale for part in work[g]], axis=1))
        ready = ahead
    return jnp.concatenate(done, axis=0)


def split(x):
    first = x.astype(jnp.bfloat16)
    rest = x - first.astype(f32)
    second = rest.astype(jnp.bfloat16)
    return first, second, (rest - second.astype(f32)).astype(jnp.bfloat16)


LEFT = (0, 0, 1, 0, 1, 2)
RIGHT = (0, 1, 0, 2, 1, 0)


def stacked(terms, order, axis):
    return jnp.concatenate([terms[i] for i in order], axis=axis)


def laced(pair):
    size = pair[0].shape[1]
    return jnp.concatenate([part[:, at : at + HALF] for at in range(0, size, HALF) for part in pair], axis=1)


def unlaced(both, side):
    size = both.shape[1]
    return jnp.concatenate([both[:, at : at + HALF] for at in range(side * HALF, size, LANES)], axis=1)


def invert_factors(gram, size):
    def columns(rows):
        lane = lax.broadcasted_iota(jnp.int32, (rows, 2 * size), 1)
        return (lane // LANES) * HALF + lane % HALF, lane % LANES < HALF

    row_column, _ = columns(PANEL)
    row_sub = lax.broadcasted_iota(jnp.int32, (PANEL, 2 * size), 0)
    part_column, part_first = columns(HALF)
    part_sub = lax.broadcasted_iota(jnp.int32, (HALF, 2 * size), 0)

    def step(index, carry):
        start = pl.multiple_of(index * PANEL, PANEL)
        stop = start + PANEL
        lanes = pl.ds(pl.multiple_of(lax.div(start, HALF) * LANES, LANES), LANES)
        block = pltpu.roll(gram[pl.ds(start, PANEL), lanes], lax.rem(LANES - lax.rem(start, HALF), LANES), 1)
        eye = (row_column - start == row_sub).astype(f32)
        within = (row_column >= start) & (row_column < stop)
        rows = eliminate(block, jnp.where(within, eye, gram[pl.ds(start, PANEL), :]))
        gram[pl.ds(start, PANEL), :] = rows

        @pl.when(stop < size)
        def _():
            right = split(rows)
            left = [jnp.where(row_column >= stop, term, jnp.zeros_like(term)) for term in right]
            change = dot16(stacked(left, LEFT, 0), stacked(right, RIGHT, 0), 0, 0)
            done = (part_column >= start) & (part_column < stop)
            for part in range(size // HALF):
                at = part * LANES
                own = jnp.where(part_first, change[at : at + HALF, :], change[at + HALF : at + LANES, :])
                held = pl.ds(part * HALF, HALF)
                gram[held, :] = jnp.where(done & (part * HALF + part_sub >= stop), 0.0, gram[held, :]) - own

        return carry

    lax.fori_loop(0, size // PANEL, step, 0)


def take_grams(rows, top_ref, low_ref, cross_ref, norm_ref):
    top = top_ref[rows, :]
    low = low_ref[rows, :]
    cross_ref[...] += dot16(top, low, 0, 0)
    top = top.astype(f32)
    low = low.astype(f32)
    norm_ref[0:1, :] += jnp.sum(top * top, axis=0, keepdims=True)
    norm_ref[SUB : SUB + 1, :] += jnp.sum(low * low, axis=0, keepdims=True)


def rotate(refs, outs, scratch, sems):
    top_ref, low_ref = refs
    low_out, inv_out, mix_out = outs
    cross_ref, norm_ref, gram, new_ref, inv_ref, mix_ref = scratch
    indiv, size = top_ref.shape
    norm_top = dot(norm_ref[0:SUB, :], jnp.ones((SUB, size), f32), 0, 0)
    norm_low = norm_ref[SUB : SUB + 1, :]
    coupling = 2.0 * cross_ref[...] / (norm_top + norm_low + epsilon)
    eye = identity(size)
    gram[...] = laced((eye + dot(coupling, coupling, 1, 1), eye + dot(coupling, coupling, 0, 0)))
    invert_factors(gram, size)
    below = lax.broadcasted_iota(jnp.int32, (size, size), 0) >= lax.broadcasted_iota(jnp.int32, (size, size), 1)
    inverse1 = jnp.where(below, unlaced(gram[...], 0), 0.0)
    inverse2 = jnp.where(below, unlaced(gram[...], 1), 0.0)
    from_top = dot(coupling, inverse2, 1, 1).astype(jnp.bfloat16)
    from_low = inverse2.astype(jnp.bfloat16)
    count = indiv // CHUNK

    def sent(step):
        rows = pl.ds(pl.multiple_of(step * CHUNK, CHUNK), CHUNK)
        return pltpu.make_async_copy(new_ref.at[rows, :], low_out.at[rows, :], sems.at[step])

    def apply(step, carry):
        rows = pl.ds(pl.multiple_of(step * CHUNK, CHUNK), CHUNK)
        new_ref[rows, :] = (
            dot16(top_ref[rows, :], from_top, 1, 0) + dot16(low_ref[rows, :], from_low, 1, 1)
        ).astype(jnp.bfloat16)
        sent(step).start()
        return carry

    lax.fori_loop(0, count, apply, 0)
    inv_ref[...] = inverse1.astype(jnp.bfloat16)
    mix_ref[...] = (-dot(inverse1, coupling, 1, 0)).astype(jnp.bfloat16)
    small = [
        pltpu.make_async_copy(inv_ref, inv_out, sems.at[count]),
        pltpu.make_async_copy(mix_ref, mix_out, sems.at[count + 1]),
    ]
    for copy in small:
        copy.start()
    for step in range(count):
        sent(step).wait()
    for copy in small:
        copy.wait()


def scratch_of(indiv, size):
    block = pltpu.VMEM((indiv, size), jnp.bfloat16)
    small = pltpu.VMEM((size, size), jnp.bfloat16)
    count = indiv // CHUNK
    return [
        block,
        block,
        pltpu.VMEM((size, size), f32),
        pltpu.VMEM((2 * SUB, size), f32),
        pltpu.VMEM((size, 2 * size), f32),
        block,
        small,
        small,
        pltpu.SemaphoreType.DMA((count + 2,)),
        pltpu.SemaphoreType.DMA((2 * count,)),
    ]


def cost(indiv, size):
    return pl.CostEstimate(flops=40 * indiv * size * size, bytes_accessed=16 * indiv * size, transcendentals=0)


def start_low(lows, copy_of):
    for core, low_hbm in enumerate(lows):
        if len(lows) == 1:
            copy_of(low_hbm).start()
        else:

            @pl.when(lax.axis_index("group") % 2 == core)
            def _():
                copy_of(low_hbm).start()


def round_kernel(lows, top_hbm, *refs):
    lows, refs = refs[:lows], refs[lows:]
    low_out, inv_out, mix_out, top_ref, low_ref, cross_ref, norm_ref, *rest = refs
    *scratch, sems, in_sems = rest
    indiv, size = top_ref.shape
    count = indiv // CHUNK

    def fetch_top(step):
        rows = pl.ds(pl.multiple_of(step * CHUNK, CHUNK), CHUNK)
        return pltpu.make_async_copy(top_hbm.at[rows, :], top_ref.at[rows, :], in_sems.at[2 * step])

    def fetch_low(step, low_hbm=lows[0]):
        rows = pl.ds(pl.multiple_of(step * CHUNK, CHUNK), CHUNK)
        return pltpu.make_async_copy(low_hbm.at[rows, :], low_ref.at[rows, :], in_sems.at[2 * step + 1])

    for step in range(count):
        fetch_top(step).start()
        start_low(lows, functools.partial(fetch_low, step))
    cross_ref[...] = jnp.zeros_like(cross_ref)
    norm_ref[...] = jnp.zeros_like(norm_ref)

    def accumulate(step, carry):
        fetch_top(step).wait()
        fetch_low(step).wait()
        take_grams(pl.ds(pl.multiple_of(step * CHUNK, CHUNK), CHUNK), top_ref, low_ref, cross_ref, norm_ref)
        return carry

    lax.fori_loop(0, count, accumulate, 0)
    rotate((top_ref, low_ref), (low_out, inv_out, mix_out), (cross_ref, norm_ref, *scratch), sems)


def rotate_low(top, lows):
    indiv, size = top.shape
    square = jax.ShapeDtypeStruct((size, size), jnp.bfloat16)
    anywhere = pl.BlockSpec(memory_space=pl.ANY)
    return pl.pallas_call(
        functools.partial(round_kernel, len(lows)),
        in_specs=[anywhere] * (1 + len(lows)),
        out_specs=[anywhere] * 3,
        out_shape=[jax.ShapeDtypeStruct((indiv, size), jnp.bfloat16), square, square],
        scratch_shapes=scratch_of(indiv, size),
        compiler_params=pltpu.CompilerParams(vmem_limit_bytes=16 * 2**20),
        cost_estimate=cost(indiv, size),
        name="rotate_low",
    )(top, *lows)


def offsets_of(dest):
    pair = lax.axis_index("pair")
    return dest[2 * pair], dest[2 * pair + 1]


def present(offsets, value):
    return (offsets[0] == value) | (offsets[1] == value)


def side_with(offsets, value):
    return jnp.where(offsets[1] == value, 1, 0)


def cross_kernel(dest, counts_hbm, out_hbm, counts_ref, cast_ref, sems):
    indiv, size = cast_ref.shape
    steps = indiv // PIECE
    offsets = offsets_of(dest)
    core = lax.axis_index("group") % 2
    zero = jnp.where(present(offsets, 2), 2, 3)
    one = jnp.where(present(offsets, 1), 1, 2)
    column = pl.multiple_of(side_with(offsets, jnp.where(core == 0, zero, one)) * size, size)

    def fetched(step):
        rows = pl.ds(step * PIECE, PIECE)
        return pltpu.make_async_copy(
            counts_hbm.at[rows, pl.ds(column, size)], counts_ref.at[rows, :], sems.at[2 * step]
        )

    def sent(step):
        rows = pl.ds(step * PIECE, PIECE)
        return pltpu.make_async_copy(cast_ref.at[rows, :], out_hbm.at[rows, :], sems.at[2 * step + 1])

    for step in range(steps):
        fetched(step).start()
    for step in range(steps):
        rows = pl.ds(step * PIECE, PIECE)
        fetched(step).wait()
        cast_ref[rows, :] = counts_ref[rows, :].astype(cast_ref.dtype)
        sent(step).start()
    for step in range(steps):
        sent(step).wait()


def picked_cross(genotypes, dest):
    indiv, size = genotypes.shape[0], genotypes.shape[1] // 2
    return pl.pallas_call(
        cross_kernel,
        in_specs=[pl.BlockSpec(memory_space=pltpu.SMEM), pl.BlockSpec(memory_space=pl.ANY)],
        out_specs=pl.BlockSpec(memory_space=pl.ANY),
        out_shape=jax.ShapeDtypeStruct((indiv, size), jnp.bfloat16),
        scratch_shapes=[
            pltpu.VMEM((indiv, size), jnp.int32),
            pltpu.VMEM((indiv, size), jnp.bfloat16),
            pltpu.SemaphoreType.DMA((2 * (indiv // PIECE),)),
        ],
        compiler_params=pltpu.CompilerParams(vmem_limit_bytes=56 * 2**20),
        name="pick_cross",
    )(dest, genotypes)


def cast_kernel(dest, *refs):
    count = len(refs) // 2
    for counts_ref, out_ref in zip(refs[:count], refs[count:]):
        out_ref[...] = counts_ref[...].astype(out_ref.dtype)


def picked(genotypes, dest, wants):
    indiv, size = genotypes.shape[0], genotypes.shape[1] // 2
    steps = 4
    in_specs, out_specs, shapes = [], [], []
    for want in wants:
        parts = len(want((0, 0)))
        rows = indiv // steps // parts

        def place(i, dest, want=want):
            offsets = offsets_of(dest)
            value, *part = want(offsets)
            return (i + (part[0] * steps if part else 0), side_with(offsets, value))

        in_specs.append(pl.BlockSpec((rows, size), place))
        out_specs.append(pl.BlockSpec((rows, size), lambda i, dest: (i, 0)))
        shapes.append(jax.ShapeDtypeStruct((indiv // parts, size), jnp.bfloat16))
    return pl.pallas_call(
        cast_kernel,
        grid_spec=pltpu.PrefetchScalarGridSpec(
            num_scalar_prefetch=1, grid=(steps,), in_specs=in_specs, out_specs=out_specs
        ),
        out_shape=shapes,
        compiler_params=pltpu.CompilerParams(vmem_limit_bytes=16 * 2**20),
        name="pick_blocks",
    )(dest, *[genotypes] * len(wants))


def first_kernel(kinds, late, dest, *refs):
    sources = [refs[sum(kinds[:code]) : sum(kinds[: code + 1])] for code in range(len(kinds))]
    inputs = sum(kinds) + (4 if late else 0)
    low_out, inv_out, mix_out, top_scaled, low_scaled = refs[inputs : inputs + 5]
    top_ref, low_ref, cross_ref, norm_ref, *rest = refs[inputs + 5 :]
    *scratch, sems, in_sems = rest
    indiv, size = top_ref.shape
    half = indiv // 2
    count = indiv // CHUNK

    offsets = offsets_of(dest)
    if late:
        codes = (0, 1, jnp.where(present(offsets, 1), 3, 2), jnp.where(present(offsets, 2), 3, 2))
    else:
        codes = (0, 2, 3, 1)

    @pl.when(lax.axis_index("group") % 2 == (1 if late else 0))
    def _():
        for side, target in enumerate((top_ref, low_ref)):
            chosen = jnp.int32(codes[0])
            for offset in range(1, 4):
                chosen = jnp.where(offsets[side] == offset, codes[offset], chosen)
            for code, arrays in enumerate(sources):
                for part in range(2):
                    rows = pl.ds(part * half, half)
                    source = arrays[part] if len(arrays) == 2 else arrays[0].at[rows, :]

                    @pl.when(chosen == code)
                    def _():
                        pltpu.make_async_copy(source, target.at[rows, :], in_sems.at[2 * side + part]).start()

        cross_ref[...] = jnp.zeros_like(cross_ref)
        norm_ref[...] = jnp.zeros_like(norm_ref)
        for side, target in enumerate((top_ref, low_ref)):
            for part in range(2):
                rows = pl.ds(part * half, half)
                pltpu.make_async_copy(sources[0][0].at[rows, :], target.at[rows, :], in_sems.at[2 * side + part]).wait()

        def add(step, sums):
            rows = pl.ds(pl.multiple_of(step * PIECE, PIECE), PIECE)
            new = []
            for side, target in enumerate((top_ref, low_ref)):
                values = target[rows, :].reshape(PIECE // (GROUP * TALL), GROUP, TALL, size)
                for k, terms in enumerate((values, values * values)):
                    small = terms[:, 0]
                    for i in range(1, GROUP):
                        small = small + terms[:, i]
                    new.append(sums[2 * side + k] + jnp.sum(small.astype(f32), axis=0))
            return tuple(new)

        sums = lax.fori_loop(0, indiv // PIECE, add, (jnp.zeros((TALL, size), f32),) * 4)
        sums = [jnp.sum(part, axis=0, keepdims=True) for part in sums]
        scales = []
        for total, squares in (sums[0:2], sums[2:4]):
            whole = total.astype(jnp.int32)
            spread = indiv * squares.astype(jnp.int32) - whole * whole
            variance = spread.astype(f32) * (1.0 / (indiv * indiv))
            scales.append((total * (1.0 / indiv), 1.0 / jnp.sqrt(variance + epsilon)))

        def kept(step):
            rows = pl.ds(pl.multiple_of(step * CHUNK, CHUNK), CHUNK)
            return [
                pltpu.make_async_copy(target.at[rows, :], scaled.at[rows, :], in_sems.at[4 + 2 * step + side])
                for side, (target, scaled) in enumerate(((top_ref, top_scaled), (low_ref, low_scaled)))
            ]

        def scale_rows(step, carry):
            rows = pl.ds(pl.multiple_of(step * CHUNK, CHUNK), CHUNK)
            for (mean, scale), target in zip(scales, (top_ref, low_ref)):
                target[rows, :] = ((target[rows, :].astype(f32) - mean) * scale).astype(jnp.bfloat16)
            for copy in kept(step):
                copy.start()
            take_grams(rows, top_ref, low_ref, cross_ref, norm_ref)
            return carry

        lax.fori_loop(0, count, scale_rows, 0)
        rotate((top_ref, low_ref), (low_out, inv_out, mix_out), (cross_ref, norm_ref, *scratch), sems)
        for step in range(count):
            for copy in kept(step):
                copy.wait()


def first_round(dest, arrays, held=()):
    indiv, size = arrays[0][0].shape
    sources = [array for source in arrays for array in source]
    block = jax.ShapeDtypeStruct((indiv, size), jnp.bfloat16)
    square = jax.ShapeDtypeStruct((size, size), jnp.bfloat16)
    anywhere = pl.BlockSpec(memory_space=pl.ANY)
    scratch = scratch_of(indiv, size)
    scratch[-1] = pltpu.SemaphoreType.DMA((2 * (indiv // CHUNK) + 4,))
    return pl.pallas_call(
        functools.partial(first_kernel, tuple(len(source) for source in arrays), bool(held)),
        in_specs=[pl.BlockSpec(memory_space=pltpu.SMEM)] + [anywhere] * (len(sources) + len(held)),
        out_specs=[anywhere] * 5,
        out_shape=[block, square, square, block, block],
        input_output_aliases={1 + len(sources) + i: 1 + i for i in range(len(held))},
        scratch_shapes=scratch,
        compiler_params=pltpu.CompilerParams(vmem_limit_bytes=16 * 2**20),
        cost_estimate=cost(indiv, size),
        name="first_round",
    )(dest, *sources, *held)


def top_kernel(lows, top_hbm, *refs):
    lows, refs = refs[:lows], refs[lows:]
    inv_hbm, mix_hbm, out_hbm, top_ref, low_ref, inv_ref, mix_ref, new_ref, sems = refs
    indiv, size = top_ref.shape
    count = indiv // CHUNK
    small = [
        pltpu.make_async_copy(inv_hbm, inv_ref, sems.at[3 * count]),
        pltpu.make_async_copy(mix_hbm, mix_ref, sems.at[3 * count + 1]),
    ]
    for copy in small:
        copy.start()

    def fetch_top(step):
        rows = pl.ds(pl.multiple_of(step * CHUNK, CHUNK), CHUNK)
        return pltpu.make_async_copy(top_hbm.at[rows, :], top_ref.at[rows, :], sems.at[3 * step])

    def fetch_low(step, low_hbm=lows[0]):
        rows = pl.ds(pl.multiple_of(step * CHUNK, CHUNK), CHUNK)
        return pltpu.make_async_copy(low_hbm.at[rows, :], low_ref.at[rows, :], sems.at[3 * step + 1])

    def sent(step):
        rows = pl.ds(pl.multiple_of(step * CHUNK, CHUNK), CHUNK)
        return pltpu.make_async_copy(new_ref.at[rows, :], out_hbm.at[rows, 0:size], sems.at[3 * step + 2])

    for step in range(count):
        fetch_top(step).start()
        start_low(lows, functools.partial(fetch_low, step))
    for copy in small:
        copy.wait()

    def apply(step, carry):
        fetch_top(step).wait()
        fetch_low(step).wait()
        rows = pl.ds(pl.multiple_of(step * CHUNK, CHUNK), CHUNK)
        new_ref[rows, :] = (
            dot16(top_ref[rows, :], inv_ref[...], 1, 1) + dot16(low_ref[rows, :], mix_ref[...], 1, 1)
        ).astype(jnp.bfloat16)
        sent(step).start()
        return carry

    lax.fori_loop(0, count, apply, 0)
    for step in range(count):
        sent(step).wait()


def rotate_top(top, lows, inverse, mix, blocks=1):
    indiv, size = top.shape
    anywhere = pl.BlockSpec(memory_space=pl.ANY)
    block = pltpu.VMEM((indiv, size), jnp.bfloat16)
    small = pltpu.VMEM((size, size), jnp.bfloat16)
    return pl.pallas_call(
        functools.partial(top_kernel, len(lows)),
        in_specs=[anywhere] * (3 + len(lows)),
        out_specs=anywhere,
        out_shape=jax.ShapeDtypeStruct((indiv, blocks * size), jnp.bfloat16),
        scratch_shapes=[block, block, small, small, block, pltpu.SemaphoreType.DMA((3 * (indiv // CHUNK) + 2,))],
        compiler_params=pltpu.CompilerParams(vmem_limit_bytes=12 * 2**20),
        cost_estimate=pl.CostEstimate(
            flops=4 * indiv * size * size, bytes_accessed=6 * indiv * size, transcendentals=0
        ),
        name="rotate_top",
    )(top, *lows, inverse, mix)


def place_kernel(low_hbm, held_ref, out_hbm, low_ref, sems):
    indiv, size = low_ref.shape
    count = indiv // PIECE
    into, out = [], []
    for step in range(count):
        rows = pl.ds(step * PIECE, PIECE)
        into.append(pltpu.make_async_copy(low_hbm.at[rows, :], low_ref.at[rows, :], sems.at[2 * step]))
        out.append(
            pltpu.make_async_copy(low_ref.at[rows, :], out_hbm.at[rows, size : 2 * size], sems.at[2 * step + 1])
        )
        into[-1].start()
    for step in range(count):
        into[step].wait()
        out[step].start()
    for copy in out:
        copy.wait()


def place_low(low, held):
    indiv, size = low.shape
    anywhere = pl.BlockSpec(memory_space=pl.ANY)
    return pl.pallas_call(
        place_kernel,
        in_specs=[anywhere] * 2,
        out_specs=anywhere,
        out_shape=jax.ShapeDtypeStruct(held.shape, held.dtype),
        input_output_aliases={1: 0},
        scratch_shapes=[
            pltpu.VMEM((indiv, size), jnp.bfloat16),
            pltpu.SemaphoreType.DMA((2 * (indiv // PIECE),)),
        ],
        compiler_params=pltpu.CompilerParams(vmem_limit_bytes=4 * 2**20),
        name="place_low",
    )(low, held)


def next_pair(array, core):
    groups, pairs = lax.axis_size("group"), lax.axis_size("pair")
    hops = []
    for group in range(groups):
        for pair in range(pairs):
            to = (pair + 1) % pairs if group % 2 == core else pair
            hops.append((group * pairs + pair, group * pairs + to))
    return lax.ppermute(array, ("group", "pair"), hops)


def regrouped_first_round(genotypes, dest_group):
    num_groups = lax.axis_size("group")
    core = lax.axis_index("group") % 2
    offsets = offsets_of(dest_group)

    def by_core(zero, one):
        return jnp.where(lax.axis_index("group") % 2 == 0, zero, one)

    def sent(array, hops):
        return lax.ppermute(array, "group", [hop for chip in range(0, num_groups, 2) for hop in hops(chip)])

    def far(chip):
        return (chip + 2) % num_groups

    cross = picked_cross(genotypes, dest_group)
    cross_one = sent(cross, lambda chip: [(chip + 1, far(chip)), (chip, chip + 1)])
    cross_zero = sent(cross, lambda chip: [(chip, far(chip)), (chip + 1, chip + 1)])
    table, _ = lax.optimization_barrier((genotypes, cross))
    near, own, lent, kept = picked(
        table,
        dest_group,
        [
            lambda o: (by_core(1, 3),),
            lambda o: (0,),
            lambda o: (by_core(3, 2), by_core(1, 0)),
            lambda o: (by_core(3, 2), by_core(0, 1)),
        ],
    )
    lent = sent(lent, lambda chip: [(chip, chip + 1), (chip + 1, chip)])
    near = sent(near, lambda chip: [(chip, chip + 1), (chip + 1, chip)])
    last = jnp.where(jnp.where(present(offsets, 3), core == 0, core == 1), kept, lent)
    last, cross_one, cross_zero = lax.optimization_barrier((last, cross_one, cross_zero))
    upper = sent(last, lambda chip: [(chip, far(chip) + 1), (chip + 1, chip)])
    lower = sent(last, lambda chip: [(chip + 1, far(chip) + 1), (chip, chip)])
    half = cross.shape[0] // 2
    passed = lax.optimization_barrier(jnp.where(present(offsets, 2), cross_one, cross_zero))
    passed = [passed[:half], passed[half:]]
    passed = [sent(part, lambda chip: [(chip, chip + 1), (chip + 1, chip)]) for part in passed]
    low_zero, *held = first_round(dest_group, ((own,), (near,), (cross_one,), (cross_zero,)))
    low_zero, held[0] = lax.optimization_barrier((low_zero, held[0]))
    low_zero = next_pair(low_zero, 0)
    upper, lower, held[0] = lax.optimization_barrier((upper, lower, held[0]))
    low_one, *held = first_round(dest_group, ((own,), (near,), passed, (upper, lower)), held)
    return (low_zero, next_pair(low_one, 1)), *held


def body(genotypes, dest_group):
    low_next, inverse, mix, top, low = regrouped_first_round(genotypes, dest_group)
    top = rotate_top(top, (low,), inverse, mix)
    for cycle_round in range(1, ROUNDS):
        low_new, inverse, mix = rotate_low(top, low_next)
        low, low_next = low_next, (passed_along(low_new, "pair", 1),)
        if cycle_round < ROUNDS - 1:
            top = rotate_top(top, low, inverse, mix)
    return place_low(low_next[0], rotate_top(top, low, inverse, mix, 2))


def solution(mesh):
    in_specs = (P(None, ("group", "pair")), P())
    out_specs = P(None, ("group", "pair"))
    return jax.shard_map(body, mesh=mesh, in_specs=in_specs, out_specs=out_specs, check_vma=False)
```

```python
import functools

import jax
import jax.numpy as jnp
from jax import lax
from jax.experimental import pallas as pl
from jax.experimental.pallas import tpu as pltpu
from jax.sharding import PartitionSpec as P

ROUNDS = 3
SUB = 8
PANEL = 32
LANES = 128
HALF = LANES // 2
CHUNK = 2048
PIECE = 512
TALL = 16
GROUP = 32

epsilon = 1e-05
f32 = jnp.float32


def passed_along(array, axis, by):
    size = lax.axis_size(axis)
    return lax.ppermute(array, axis, [(i, (i + by) % size) for i in range(size)])


def dot(a, b, ca, cb):
    return lax.dot_general(
        a, b, (((ca,), (cb,)), ((), ())), precision=lax.Precision.HIGHEST, preferred_element_type=f32
    )


def dot16(a, b, ca, cb):
    return lax.dot_general(a, b, (((ca,), (cb,)), ((), ())), preferred_element_type=f32)


def identity(size):
    rows = lax.broadcasted_iota(jnp.int32, (size, size), 0)
    cols = lax.broadcasted_iota(jnp.int32, (size, size), 1)
    return (rows == cols).astype(f32)


def eliminate(block, rows):
    tile = (SUB, LANES)
    count = PANEL // SUB
    wide = rows.shape[1] // LANES
    first = lax.broadcasted_iota(jnp.int32, tile, 1) < HALF
    sub = lax.broadcasted_iota(jnp.int32, tile, 0)

    def down(value, j):
        return jnp.broadcast_to(value[j : j + 1, :], tile)

    def along(value, k):
        return jnp.where(
            first,
            jnp.broadcast_to(value[:, k : k + 1], tile),
            jnp.broadcast_to(value[:, HALF + k : HALF + k + 1], tile),
        )

    block = [block[SUB * t : SUB * t + SUB, :] for t in range(count)]
    work = [
        [rows[SUB * t : SUB * t + SUB, LANES * w : LANES * w + LANES] for w in range(wide)] for t in range(count)
    ]
    done = []
    ready = [[along(part, k) for part in block] for k in range(SUB)]
    for g in range(count):
        later = SUB * (g + 1)
        ahead = []
        if g + 1 < count:
            ahead = [[None] * (g + 1) + [along(part, later + k) for part in block[g + 1 :]] for k in range(SUB)]
        head = {(m, l): down(ready[l][g], m) for l in range(SUB) for m in range(l, SUB)}
        pivots = head[0, 0]
        for j in range(SUB):
            pivot = head[j, j]
            if j:
                pivots = jnp.where(sub == j, pivot, pivots)
            guess = pl.reciprocal(pivot, approx=True)
            mend = 2.0 - pivot * guess
            inverse = guess * mend
            for l in range(j + 1, SUB):
                for m in range(l, SUB):
                    head[m, l] = head[m, l] - (head[l, j] * head[m, j]) * guess * mend
            own = [down(part, j) for part in work[g]]
            own_block = down(block[g], j)
            for t in range(g, count):
                factor = ready[j][t] * inverse
                if t == g:
                    factor = jnp.where(sub > j, factor, 0.0)
                for m in range(j + 1, SUB):
                    ready[m][t] = ready[m][t] - factor * head[m, j]
                if t > g:
                    for k, column in enumerate(ahead):
                        column[t] = column[t] - factor * down(ready[j][g + 1], k)
                block[t] = block[t] - factor * own_block
                work[t] = [part - factor * spread for part, spread in zip(work[t], own)]
        scale = lax.rsqrt(pivots)
        done.append(jnp.concatenate([part * scale for part in work[g]], axis=1))
        ready = ahead
    return jnp.concatenate(done, axis=0)


def split(x):
    first = x.astype(jnp.bfloat16)
    rest = x - first.astype(f32)
    second = rest.astype(jnp.bfloat16)
    return first, second, (rest - second.astype(f32)).astype(jnp.bfloat16)


LEFT = (0, 0, 1, 0, 1, 2)
RIGHT = (0, 1, 0, 2, 1, 0)


def stacked(terms, order, axis):
    return jnp.concatenate([terms[i] for i in order], axis=axis)


def laced(pair):
    size = pair[0].shape[1]
    return jnp.concatenate([part[:, at : at + HALF] for at in range(0, size, HALF) for part in pair], axis=1)


def unlaced(both, side):
    size = both.shape[1]
    return jnp.concatenate([both[:, at : at + HALF] for at in range(side * HALF, size, LANES)], axis=1)


def invert_factors(gram, size):
    def columns(rows):
        lane = lax.broadcasted_iota(jnp.int32, (rows, 2 * size), 1)
        return (lane // LANES) * HALF + lane % HALF, lane % LANES < HALF

    row_column, _ = columns(PANEL)
    row_sub = lax.broadcasted_iota(jnp.int32, (PANEL, 2 * size), 0)
    part_column, part_first = columns(HALF)
    part_sub = lax.broadcasted_iota(jnp.int32, (HALF, 2 * size), 0)

    def step(index, carry):
        start = pl.multiple_of(index * PANEL, PANEL)
        stop = start + PANEL
        lanes = pl.ds(pl.multiple_of(lax.div(start, HALF) * LANES, LANES), LANES)
        block = pltpu.roll(gram[pl.ds(start, PANEL), lanes], lax.rem(LANES - lax.rem(start, HALF), LANES), 1)
        eye = (row_column - start == row_sub).astype(f32)
        within = (row_column >= start) & (row_column < stop)
        rows = eliminate(block, jnp.where(within, eye, gram[pl.ds(start, PANEL), :]))
        gram[pl.ds(start, PANEL), :] = rows

        @pl.when(stop < size)
        def _():
            right = split(rows)
            left = [jnp.where(row_column >= stop, term, jnp.zeros_like(term)) for term in right]
            change = dot16(stacked(left, LEFT, 0), stacked(right, RIGHT, 0), 0, 0)
            done = (part_column >= start) & (part_column < stop)
            for part in range(size // HALF):
                at = part * LANES
                own = jnp.where(part_first, change[at : at + HALF, :], change[at + HALF : at + LANES, :])
                held = pl.ds(part * HALF, HALF)
                gram[held, :] = jnp.where(done & (part * HALF + part_sub >= stop), 0.0, gram[held, :]) - own

        return carry

    lax.fori_loop(0, size // PANEL, step, 0)


def take_grams(rows, top_ref, low_ref, cross_ref, norm_ref):
    top = top_ref[rows, :]
    low = low_ref[rows, :]
    cross_ref[...] += dot16(top, low, 0, 0)
    top = top.astype(f32)
    low = low.astype(f32)
    norm_ref[0:1, :] += jnp.sum(top * top, axis=0, keepdims=True)
    norm_ref[SUB : SUB + 1, :] += jnp.sum(low * low, axis=0, keepdims=True)


def rotate(refs, outs, scratch, sems):
    top_ref, low_ref = refs
    low_out, inv_out, mix_out = outs
    cross_ref, norm_ref, gram, new_ref, inv_ref, mix_ref = scratch
    indiv, size = top_ref.shape
    norm_top = dot(norm_ref[0:SUB, :], jnp.ones((SUB, size), f32), 0, 0)
    norm_low = norm_ref[SUB : SUB + 1, :]
    coupling = 2.0 * cross_ref[...] / (norm_top + norm_low + epsilon)
    eye = identity(size)
    gram[...] = laced((eye + dot(coupling, coupling, 1, 1), eye + dot(coupling, coupling, 0, 0)))
    invert_factors(gram, size)
    below = lax.broadcasted_iota(jnp.int32, (size, size), 0) >= lax.broadcasted_iota(jnp.int32, (size, size), 1)
    inverse1 = jnp.where(below, unlaced(gram[...], 0), 0.0)
    inverse2 = jnp.where(below, unlaced(gram[...], 1), 0.0)
    from_top = dot(coupling, inverse2, 1, 1).astype(jnp.bfloat16)
    from_low = inverse2.astype(jnp.bfloat16)
    count = indiv // CHUNK

    def sent(step):
        rows = pl.ds(pl.multiple_of(step * CHUNK, CHUNK), CHUNK)
        return pltpu.make_async_copy(new_ref.at[rows, :], low_out.at[rows, :], sems.at[step])

    def apply(step, carry):
        rows = pl.ds(pl.multiple_of(step * CHUNK, CHUNK), CHUNK)
        new_ref[rows, :] = (
            dot16(top_ref[rows, :], from_top, 1, 0) + dot16(low_ref[rows, :], from_low, 1, 1)
        ).astype(jnp.bfloat16)
        sent(step).start()
        return carry

    lax.fori_loop(0, count, apply, 0)
    inv_ref[...] = inverse1.astype(jnp.bfloat16)
    mix_ref[...] = (-dot(inverse1, coupling, 1, 0)).astype(jnp.bfloat16)
    small = [
        pltpu.make_async_copy(inv_ref, inv_out, sems.at[count]),
        pltpu.make_async_copy(mix_ref, mix_out, sems.at[count + 1]),
    ]
    for copy in small:
        copy.start()
    for step in range(count):
        sent(step).wait()
    for copy in small:
        copy.wait()


def scratch_of(indiv, size):
    block = pltpu.VMEM((indiv, size), jnp.bfloat16)
    small = pltpu.VMEM((size, size), jnp.bfloat16)
    count = indiv // CHUNK
    return [
        block,
        block,
        pltpu.VMEM((size, size), f32),
        pltpu.VMEM((2 * SUB, size), f32),
        pltpu.VMEM((size, 2 * size), f32),
        block,
        small,
        small,
        pltpu.SemaphoreType.DMA((count + 2,)),
        pltpu.SemaphoreType.DMA((2 * count,)),
    ]


def cost(indiv, size):
    return pl.CostEstimate(flops=40 * indiv * size * size, bytes_accessed=16 * indiv * size, transcendentals=0)


def start_low(lows, copy_of):
    for core, low_hbm in enumerate(lows):
        if len(lows) == 1:
            copy_of(low_hbm).start()
        else:

            @pl.when(lax.axis_index("group") % 2 == core)
            def _():
                copy_of(low_hbm).start()


def round_kernel(lows, top_hbm, *refs):
    lows, refs = refs[:lows], refs[lows:]
    low_out, inv_out, mix_out, top_ref, low_ref, cross_ref, norm_ref, *rest = refs
    *scratch, sems, in_sems = rest
    indiv, size = top_ref.shape
    count = indiv // CHUNK

    def fetch_top(step):
        rows = pl.ds(pl.multiple_of(step * CHUNK, CHUNK), CHUNK)
        return pltpu.make_async_copy(top_hbm.at[rows, :], top_ref.at[rows, :], in_sems.at[2 * step])

    def fetch_low(step, low_hbm=lows[0]):
        rows = pl.ds(pl.multiple_of(step * CHUNK, CHUNK), CHUNK)
        return pltpu.make_async_copy(low_hbm.at[rows, :], low_ref.at[rows, :], in_sems.at[2 * step + 1])

    for step in range(count):
        fetch_top(step).start()
        start_low(lows, functools.partial(fetch_low, step))
    cross_ref[...] = jnp.zeros_like(cross_ref)
    norm_ref[...] = jnp.zeros_like(norm_ref)

    def accumulate(step, carry):
        fetch_top(step).wait()
        fetch_low(step).wait()
        take_grams(pl.ds(pl.multiple_of(step * CHUNK, CHUNK), CHUNK), top_ref, low_ref, cross_ref, norm_ref)
        return carry

    lax.fori_loop(0, count, accumulate, 0)
    rotate((top_ref, low_ref), (low_out, inv_out, mix_out), (cross_ref, norm_ref, *scratch), sems)


def rotate_low(top, lows):
    indiv, size = top.shape
    square = jax.ShapeDtypeStruct((size, size), jnp.bfloat16)
    anywhere = pl.BlockSpec(memory_space=pl.ANY)
    return pl.pallas_call(
        functools.partial(round_kernel, len(lows)),
        in_specs=[anywhere] * (1 + len(lows)),
        out_specs=[anywhere] * 3,
        out_shape=[jax.ShapeDtypeStruct((indiv, size), jnp.bfloat16), square, square],
        scratch_shapes=scratch_of(indiv, size),
        compiler_params=pltpu.CompilerParams(vmem_limit_bytes=16 * 2**20),
        cost_estimate=cost(indiv, size),
        name="rotate_low",
    )(top, *lows)


def offsets_of(dest):
    pair = lax.axis_index("pair")
    return dest[2 * pair], dest[2 * pair + 1]


def present(offsets, value):
    return (offsets[0] == value) | (offsets[1] == value)


def side_with(offsets, value):
    return jnp.where(offsets[1] == value, 1, 0)


def cross_kernel(dest, counts_hbm, out_hbm, counts_ref, cast_ref, sems):
    indiv, size = cast_ref.shape
    steps = indiv // PIECE
    offsets = offsets_of(dest)
    core = lax.axis_index("group") % 2
    zero = jnp.where(present(offsets, 2), 2, 3)
    one = jnp.where(present(offsets, 1), 1, 2)
    column = pl.multiple_of(side_with(offsets, jnp.where(core == 0, zero, one)) * size, size)

    def fetched(step):
        rows = pl.ds(step * PIECE, PIECE)
        return pltpu.make_async_copy(
            counts_hbm.at[rows, pl.ds(column, size)], counts_ref.at[rows, :], sems.at[2 * step]
        )

    def sent(step):
        rows = pl.ds(step * PIECE, PIECE)
        return pltpu.make_async_copy(cast_ref.at[rows, :], out_hbm.at[rows, :], sems.at[2 * step + 1])

    for step in range(steps):
        fetched(step).start()
    for step in range(steps):
        rows = pl.ds(step * PIECE, PIECE)
        fetched(step).wait()
        cast_ref[rows, :] = counts_ref[rows, :].astype(cast_ref.dtype)
        sent(step).start()
    for step in range(steps):
        sent(step).wait()


def picked_cross(genotypes, dest):
    indiv, size = genotypes.shape[0], genotypes.shape[1] // 2
    return pl.pallas_call(
        cross_kernel,
        in_specs=[pl.BlockSpec(memory_space=pltpu.SMEM), pl.BlockSpec(memory_space=pl.ANY)],
        out_specs=pl.BlockSpec(memory_space=pl.ANY),
        out_shape=jax.ShapeDtypeStruct((indiv, size), jnp.bfloat16),
        scratch_shapes=[
            pltpu.VMEM((indiv, size), jnp.int32),
            pltpu.VMEM((indiv, size), jnp.bfloat16),
            pltpu.SemaphoreType.DMA((2 * (indiv // PIECE),)),
        ],
        compiler_params=pltpu.CompilerParams(vmem_limit_bytes=56 * 2**20),
        name="pick_cross",
    )(dest, genotypes)


def cast_kernel(dest, *refs):
    count = len(refs) // 2
    for counts_ref, out_ref in zip(refs[:count], refs[count:]):
        out_ref[...] = counts_ref[...].astype(out_ref.dtype)


def picked(genotypes, dest, wants):
    indiv, size = genotypes.shape[0], genotypes.shape[1] // 2
    steps = 4
    in_specs, out_specs, shapes = [], [], []
    for want in wants:
        parts = len(want((0, 0)))
        rows = indiv // steps // parts

        def place(i, dest, want=want):
            offsets = offsets_of(dest)
            value, *part = want(offsets)
            return (i + (part[0] * steps if part else 0), side_with(offsets, value))

        in_specs.append(pl.BlockSpec((rows, size), place))
        out_specs.append(pl.BlockSpec((rows, size), lambda i, dest: (i, 0)))
        shapes.append(jax.ShapeDtypeStruct((indiv // parts, size), jnp.bfloat16))
    return pl.pallas_call(
        cast_kernel,
        grid_spec=pltpu.PrefetchScalarGridSpec(
            num_scalar_prefetch=1, grid=(steps,), in_specs=in_specs, out_specs=out_specs
        ),
        out_shape=shapes,
        compiler_params=pltpu.CompilerParams(vmem_limit_bytes=16 * 2**20),
        name="pick_blocks",
    )(dest, *[genotypes] * len(wants))


def first_kernel(kinds, late, dest, *refs):
    sources = [refs[sum(kinds[:code]) : sum(kinds[: code + 1])] for code in range(len(kinds))]
    inputs = sum(kinds) + (4 if late else 0)
    low_out, inv_out, mix_out, top_scaled, low_scaled = refs[inputs : inputs + 5]
    top_ref, low_ref, cross_ref, norm_ref, *rest = refs[inputs + 5 :]
    *scratch, sems, in_sems = rest
    indiv, size = top_ref.shape
    half = indiv // 2
    count = indiv // CHUNK

    offsets = offsets_of(dest)
    if late:
        codes = (0, 1, jnp.where(present(offsets, 1), 3, 2), jnp.where(present(offsets, 2), 3, 2))
    else:
        codes = (0, 2, 3, 1)

    @pl.when(lax.axis_index("group") % 2 == (1 if late else 0))
    def _():
        for side, target in enumerate((top_ref, low_ref)):
            chosen = jnp.int32(codes[0])
            for offset in range(1, 4):
                chosen = jnp.where(offsets[side] == offset, codes[offset], chosen)
            for code, arrays in enumerate(sources):
                for part in range(2):
                    rows = pl.ds(part * half, half)
                    source = arrays[part] if len(arrays) == 2 else arrays[0].at[rows, :]

                    @pl.when(chosen == code)
                    def _():
                        pltpu.make_async_copy(source, target.at[rows, :], in_sems.at[2 * side + part]).start()

        cross_ref[...] = jnp.zeros_like(cross_ref)
        norm_ref[...] = jnp.zeros_like(norm_ref)
        for side, target in enumerate((top_ref, low_ref)):
            for part in range(2):
                rows = pl.ds(part * half, half)
                pltpu.make_async_copy(sources[0][0].at[rows, :], target.at[rows, :], in_sems.at[2 * side + part]).wait()

        def add(step, sums):
            rows = pl.ds(pl.multiple_of(step * PIECE, PIECE), PIECE)
            new = []
            for side, target in enumerate((top_ref, low_ref)):
                values = target[rows, :].reshape(PIECE // (GROUP * TALL), GROUP, TALL, size)
                for k, terms in enumerate((values, values * values)):
                    small = terms[:, 0]
                    for i in range(1, GROUP):
                        small = small + terms[:, i]
                    new.append(sums[2 * side + k] + jnp.sum(small.astype(f32), axis=0))
            return tuple(new)

        sums = lax.fori_loop(0, indiv // PIECE, add, (jnp.zeros((TALL, size), f32),) * 4)
        sums = [jnp.sum(part, axis=0, keepdims=True) for part in sums]
        scales = []
        for total, squares in (sums[0:2], sums[2:4]):
            whole = total.astype(jnp.int32)
            spread = indiv * squares.astype(jnp.int32) - whole * whole
            variance = spread.astype(f32) * (1.0 / (indiv * indiv))
            scales.append((total * (1.0 / indiv), 1.0 / jnp.sqrt(variance + epsilon)))

        def kept(step):
            rows = pl.ds(pl.multiple_of(step * CHUNK, CHUNK), CHUNK)
            return [
                pltpu.make_async_copy(target.at[rows, :], scaled.at[rows, :], in_sems.at[4 + 2 * step + side])
                for side, (target, scaled) in enumerate(((top_ref, top_scaled), (low_ref, low_scaled)))
            ]

        def scale_rows(step, carry):
            rows = pl.ds(pl.multiple_of(step * CHUNK, CHUNK), CHUNK)
            for (mean, scale), target in zip(scales, (top_ref, low_ref)):
                target[rows, :] = ((target[rows, :].astype(f32) - mean) * scale).astype(jnp.bfloat16)
            take_grams(rows, top_ref, low_ref, cross_ref, norm_ref)
            return carry

        lax.fori_loop(0, count, scale_rows, 0)
        for step in range(count):
            for copy in kept(step):
                copy.start()
        rotate((top_ref, low_ref), (low_out, inv_out, mix_out), (cross_ref, norm_ref, *scratch), sems)
        for step in range(count):
            for copy in kept(step):
                copy.wait()


def first_round(dest, arrays, held=()):
    indiv, size = arrays[0][0].shape
    sources = [array for source in arrays for array in source]
    block = jax.ShapeDtypeStruct((indiv, size), jnp.bfloat16)
    square = jax.ShapeDtypeStruct((size, size), jnp.bfloat16)
    anywhere = pl.BlockSpec(memory_space=pl.ANY)
    scratch = scratch_of(indiv, size)
    scratch[-1] = pltpu.SemaphoreType.DMA((2 * (indiv // CHUNK) + 4,))
    return pl.pallas_call(
        functools.partial(first_kernel, tuple(len(source) for source in arrays), bool(held)),
        in_specs=[pl.BlockSpec(memory_space=pltpu.SMEM)] + [anywhere] * (len(sources) + len(held)),
        out_specs=[anywhere] * 5,
        out_shape=[block, square, square, block, block],
        input_output_aliases={1 + len(sources) + i: 1 + i for i in range(len(held))},
        scratch_shapes=scratch,
        compiler_params=pltpu.CompilerParams(vmem_limit_bytes=16 * 2**20),
        cost_estimate=cost(indiv, size),
        name="first_round",
    )(dest, *sources, *held)


def top_kernel(lows, top_hbm, *refs):
    lows, refs = refs[:lows], refs[lows:]
    inv_hbm, mix_hbm, out_hbm, top_ref, low_ref, inv_ref, mix_ref, new_ref, sems = refs
    indiv, size = top_ref.shape
    count = indiv // CHUNK
    small = [
        pltpu.make_async_copy(inv_hbm, inv_ref, sems.at[3 * count]),
        pltpu.make_async_copy(mix_hbm, mix_ref, sems.at[3 * count + 1]),
    ]
    for copy in small:
        copy.start()

    def fetch_top(step):
        rows = pl.ds(pl.multiple_of(step * CHUNK, CHUNK), CHUNK)
        return pltpu.make_async_copy(top_hbm.at[rows, :], top_ref.at[rows, :], sems.at[3 * step])

    def fetch_low(step, low_hbm=lows[0]):
        rows = pl.ds(pl.multiple_of(step * CHUNK, CHUNK), CHUNK)
        return pltpu.make_async_copy(low_hbm.at[rows, :], low_ref.at[rows, :], sems.at[3 * step + 1])

    def sent(step):
        rows = pl.ds(pl.multiple_of(step * CHUNK, CHUNK), CHUNK)
        return pltpu.make_async_copy(new_ref.at[rows, :], out_hbm.at[rows, 0:size], sems.at[3 * step + 2])

    for step in range(count):
        fetch_top(step).start()
        start_low(lows, functools.partial(fetch_low, step))
    for copy in small:
        copy.wait()

    def apply(step, carry):
        fetch_top(step).wait()
        fetch_low(step).wait()
        rows = pl.ds(pl.multiple_of(step * CHUNK, CHUNK), CHUNK)
        new_ref[rows, :] = (
            dot16(top_ref[rows, :], inv_ref[...], 1, 1) + dot16(low_ref[rows, :], mix_ref[...], 1, 1)
        ).astype(jnp.bfloat16)
        sent(step).start()
        return carry

    lax.fori_loop(0, count, apply, 0)
    for step in range(count):
        sent(step).wait()


def rotate_top(top, lows, inverse, mix, blocks=1):
    indiv, size = top.shape
    anywhere = pl.BlockSpec(memory_space=pl.ANY)
    block = pltpu.VMEM((indiv, size), jnp.bfloat16)
    small = pltpu.VMEM((size, size), jnp.bfloat16)
    return pl.pallas_call(
        functools.partial(top_kernel, len(lows)),
        in_specs=[anywhere] * (3 + len(lows)),
        out_specs=anywhere,
        out_shape=jax.ShapeDtypeStruct((indiv, blocks * size), jnp.bfloat16),
        scratch_shapes=[block, block, small, small, block, pltpu.SemaphoreType.DMA((3 * (indiv // CHUNK) + 2,))],
        compiler_params=pltpu.CompilerParams(vmem_limit_bytes=12 * 2**20),
        cost_estimate=pl.CostEstimate(
            flops=4 * indiv * size * size, bytes_accessed=6 * indiv * size, transcendentals=0
        ),
        name="rotate_top",
    )(top, *lows, inverse, mix)


def place_kernel(low_hbm, held_ref, out_hbm, low_ref, sems):
    indiv, size = low_ref.shape
    count = indiv // PIECE
    into, out = [], []
    for step in range(count):
        rows = pl.ds(step * PIECE, PIECE)
        into.append(pltpu.make_async_copy(low_hbm.at[rows, :], low_ref.at[rows, :], sems.at[2 * step]))
        out.append(
            pltpu.make_async_copy(low_ref.at[rows, :], out_hbm.at[rows, size : 2 * size], sems.at[2 * step + 1])
        )
        into[-1].start()
    for step in range(count):
        into[step].wait()
        out[step].start()
    for copy in out:
        copy.wait()


def place_low(low, held):
    indiv, size = low.shape
    anywhere = pl.BlockSpec(memory_space=pl.ANY)
    return pl.pallas_call(
        place_kernel,
        in_specs=[anywhere] * 2,
        out_specs=anywhere,
        out_shape=jax.ShapeDtypeStruct(held.shape, held.dtype),
        input_output_aliases={1: 0},
        scratch_shapes=[
            pltpu.VMEM((indiv, size), jnp.bfloat16),
            pltpu.SemaphoreType.DMA((2 * (indiv // PIECE),)),
        ],
        compiler_params=pltpu.CompilerParams(vmem_limit_bytes=4 * 2**20),
        name="place_low",
    )(low, held)


def next_pair(array, core):
    groups, pairs = lax.axis_size("group"), lax.axis_size("pair")
    hops = []
    for group in range(groups):
        for pair in range(pairs):
            to = (pair + 1) % pairs if group % 2 == core else pair
            hops.append((group * pairs + pair, group * pairs + to))
    return lax.ppermute(array, ("group", "pair"), hops)


def regrouped_first_round(genotypes, dest_group):
    num_groups = lax.axis_size("group")
    core = lax.axis_index("group") % 2
    offsets = offsets_of(dest_group)

    def by_core(zero, one):
        return jnp.where(lax.axis_index("group") % 2 == 0, zero, one)

    def sent(array, hops):
        return lax.ppermute(array, "group", [hop for chip in range(0, num_groups, 2) for hop in hops(chip)])

    def far(chip):
        return (chip + 2) % num_groups

    cross = picked_cross(genotypes, dest_group)
    cross_one = sent(cross, lambda chip: [(chip + 1, far(chip)), (chip, chip + 1)])
    cross_zero = sent(cross, lambda chip: [(chip, far(chip)), (chip + 1, chip + 1)])
    table, _ = lax.optimization_barrier((genotypes, cross))
    near, own, lent, kept = picked(
        table,
        dest_group,
        [
            lambda o: (by_core(1, 3),),
            lambda o: (0,),
            lambda o: (by_core(3, 2), by_core(1, 0)),
            lambda o: (by_core(3, 2), by_core(0, 1)),
        ],
    )
    lent = sent(lent, lambda chip: [(chip, chip + 1), (chip + 1, chip)])
    near = sent(near, lambda chip: [(chip, chip + 1), (chip + 1, chip)])
    last = jnp.where(jnp.where(present(offsets, 3), core == 0, core == 1), kept, lent)
    last, cross_one, cross_zero = lax.optimization_barrier((last, cross_one, cross_zero))
    upper = sent(last, lambda chip: [(chip, far(chip) + 1), (chip + 1, chip)])
    lower = sent(last, lambda chip: [(chip + 1, far(chip) + 1), (chip, chip)])
    half = cross.shape[0] // 2
    passed = lax.optimization_barrier(jnp.where(present(offsets, 2), cross_one, cross_zero))
    passed = [passed[:half], passed[half:]]
    passed = [sent(part, lambda chip: [(chip, chip + 1), (chip + 1, chip)]) for part in passed]
    low_zero, *held = first_round(dest_group, ((own,), (near,), (cross_one,), (cross_zero,)))
    low_zero, held[0] = lax.optimization_barrier((low_zero, held[0]))
    low_zero = next_pair(low_zero, 0)
    upper, lower, held[0] = lax.optimization_barrier((upper, lower, held[0]))
    low_one, *held = first_round(dest_group, ((own,), (near,), passed, (upper, lower)), held)
    return (low_zero, next_pair(low_one, 1)), *held


def body(genotypes, dest_group):
    low_next, inverse, mix, top, low = regrouped_first_round(genotypes, dest_group)
    top = rotate_top(top, (low,), inverse, mix)
    for cycle_round in range(1, ROUNDS):
        low_new, inverse, mix = rotate_low(top, low_next)
        low, low_next = low_next, (passed_along(low_new, "pair", 1),)
        if cycle_round < ROUNDS - 1:
            top = rotate_top(top, low, inverse, mix)
    return place_low(low_next[0], rotate_top(top, low, inverse, mix, 2))


def solution(mesh):
    in_specs = (P(None, ("group", "pair")), P())
    out_specs = P(None, ("group", "pair"))
    return jax.shard_map(body, mesh=mesh, in_specs=in_specs, out_specs=out_specs, check_vma=False)
```
